256 devices in a mesh: dp: 32 (over z, y), shard: 8 (over x, core).
Axes of the slice: x: 4, y: 4, z: 8, core: 2. Of those that a mesh axis runs over, the one named last changes fastest.
Arguments:
- gradient: bfloat16 [32, 3072, 3968], P('dp', 'shard'), may hold values from -6 to 6
- memory: bfloat16 [32, 3072, 3968], P('dp', 'shard'), may hold values from -4 to 4
- old_factor: bfloat16 [3968, 128], replicated, may hold values from -0.09375 to 0.09375
Outputs:
- new_memory: bfloat16 [32, 3072, 3968], P('dp', 'shard')
- new_factor: float32 [3968, 128], replicated
The draws below stay inside these ranges and needn't reach their ends.
All inputs are finite; a program needn't handle non-finite values.
Results may differ from the reference program's by a relative error of at most 0.001.
Values sent between devices are 32-bit elements; how exact they have to be, the bound alone decides.
A program may use at most 64 MiB of HBM per device.

```python
import jax
import jax.numpy as jnp
from jax import lax

D = 3968
RANK = 128
HIDDEN_SIZE = 3072
N_DP = 32


def steps_of(own_key, dims, cuts, least, largest):
    def one(dim, shards_of):
        draws = jax.random.uniform(jax.random.fold_in(jax.random.fold_in(own_key, 6), dim), (shards_of,), jnp.float32, least / len(cuts), largest / len(cuts))
        return jnp.repeat(jnp.exp(draws), dims[dim] // shards_of).reshape((-1,) + (1,) * (len(dims) - dim - 1))

    gain = one(*cuts[0])
    for cut in cuts[1:]:
        gain = gain * one(*cut)
    return gain


def noise(own_key, shape, deviation, reach, cuts=(), kind=jnp.bfloat16):
    values = deviation * jax.random.normal(own_key, shape, jnp.float32)
    if cuts:
        values = values * steps_of(own_key, shape, cuts, -0.22, 0.18)
    return jnp.clip(values, -reach, reach).astype(kind)


def setup_inputs(seed: int = 0) -> dict:
    splits = jax.random.split(jax.random.key(seed), 4)
    return {
        "gradient": noise(splits[0], (N_DP, HIDDEN_SIZE, D), 1.0, 6.0, ((0, 32), (1, 8))),
        "memory": noise(splits[1], (N_DP, HIDDEN_SIZE, D), 0.5, 4.0, ((0, 32), (1, 8))),
        "old_factor": noise(splits[2], (D, RANK), D ** -0.5, 0.09375),
    }


def corrected_at(gradient, memory, index):
    return gradient[index].astype(jnp.float32) + memory[index].astype(jnp.float32)

def reference(gradient, memory, old_factor):
    factor = old_factor.astype(jnp.float32)

    def add_span(index, total):
        rows = corrected_at(gradient, memory, index)
        return total + jnp.dot(rows, factor, precision=lax.Precision.HIGHEST)
    spanned = lax.fori_loop(0, N_DP, add_span, jnp.zeros((HIDDEN_SIZE, RANK), jnp.float32)) / N_DP
    gram_matrix = jnp.dot(spanned.T, spanned, precision=lax.Precision.HIGHEST)
    lower_factor = jnp.linalg.cholesky(gram_matrix)
    orthonormal = jax.scipy.linalg.solve_triangular(lower_factor, spanned.T, lower=True).T

    def add_factor(index, total):
        rows = corrected_at(gradient, memory, index)
        return total + jnp.einsum('hd,hk->dk', rows, orthonormal, precision=lax.Precision.HIGHEST)
    new_factor = lax.fori_loop(0, N_DP, add_factor, jnp.zeros((D, RANK), jnp.float32)) / N_DP
    decompressed = jnp.dot(orthonormal, new_factor.T, precision=lax.Precision.HIGHEST)

    def residual_of(index):
        return (corrected_at(gradient, memory, index) - decompressed).astype(jnp.bfloat16)
    new_memory = lax.map(residual_of, jnp.arange(N_DP, dtype=jnp.int32))
    return (new_memory, new_factor)
```

```python
import functools

import jax
import jax.numpy as jnp
from jax import lax
from jax.experimental import pallas as pl
from jax.experimental.pallas import tpu as pltpu
from jax.sharding import PartitionSpec as P

MESH = pl.DeviceIdType.MESH
D = 3968
RANK = 128
ROWS = 384
ZS, YS, XS, CORES = 8, 4, 4, 2
DP = ZS * YS
PIECE = ROWS // DP
PADDED = 4096
HALF = PADDED // CORES
BIG = HALF // 4
MID = BIG // 4
SMALL = MID // ZS
BLOCKS = D // 128
ORDER = (2, 1, 3, 0)
VMEM_BYTES = 48 * 1024 * 1024


def eight_columns(step, gram, inverse):
    row = lax.broadcasted_iota(jnp.int32, (RANK, 1), 0)
    row8 = lax.broadcasted_iota(jnp.int32, (8, RANK), 0)
    live = row[8:] + 8 * step < RANK
    columns = [jnp.broadcast_to(gram[:, k:k + 1], (RANK, RANK)) for k in range(8)]
    top = [column[:8] for column in columns]
    below = [jnp.where(live, column[8:], 0.0) for column in columns]
    gram8, inverse8 = gram[:8], inverse[:8]
    gram_rest, inverse_rest = gram[8:], inverse[8:]
    pivots = []
    for k in range(8):
        pivot = jnp.broadcast_to(top[k][k:k + 1], (8, RANK))
        reciprocal = 1.0 / pivot
        pivots.append(pivot[:1])
        factor8 = jnp.where(row8 > k, top[k] * reciprocal, 0.0)
        factor = below[k] * reciprocal[:1]
        for j in range(k + 1, 8):
            upper = top[j][k:k + 1]
            top[j] = top[j] - factor8 * upper
            below[j] = below[j] - factor * upper
        gram_row, inverse_row = gram8[k:k + 1], inverse8[k:k + 1]
        gram_rest = gram_rest - factor * gram_row
        inverse_rest = inverse_rest - factor * inverse_row
        gram8 = gram8 - factor8 * gram_row
        inverse8 = inverse8 - factor8 * inverse_row
    done = inverse8 * lax.rsqrt(jnp.concatenate(pivots, 0))
    inverse = jnp.concatenate([inverse_rest, done], 0)
    gram = jnp.concatenate([gram_rest, gram8], 0)
    return pltpu.roll(gram, RANK - 8, 1), inverse


def split(value):
    high = value.astype(jnp.bfloat16)
    return high, (value - high.astype(jnp.float32)).astype(jnp.bfloat16)


def land(ref, sem):
    pltpu.make_async_copy(ref, ref, sem).wait()


def exchange_kernel(g_hbm, m_hbm, f_hbm, n_ref, o_ref,
                    g, m, f, gt, mt, part, part_in, span_all, span, span2,
                    gram, gram_in, gram_x, gram_back, lower, inverse, x, core_in, a_in, b_in, z_in,
                    load_sem, part_send, part_recv, span_send, span_recv,
                    gram_send, gram_recv, core_send, core_recv, a_send, a_recv, b_send, b_recv,
                    z_send, z_recv, gz_send, gz_recv, gb_send, gb_recv, ga_send, ga_recv, gc_send, gc_recv):
    dp, shard = lax.axis_index("dp"), lax.axis_index("shard")
    zi, yi = dp // YS, dp % YS
    xi, ci = shard // CORES, shard % CORES
    a = xi * (1 - ci) + yi * ci
    b = yi * (1 - ci) + xi * ci

    def plane_peer(j):
        return (j, shard)

    def a_peer(k):
        return (zi * YS + (yi + k * ci) % 4, ((xi + k * (1 - ci)) % 4) * CORES + ci)

    def b_peer(k):
        return (zi * YS + (yi + k * (1 - ci)) % 4, ((xi + k * ci) % 4) * CORES + ci)

    def x_peer(k):
        return (dp, ((xi + k) % 4) * CORES + ci)

    def z_peer(k):
        return (((zi + k) % ZS) * YS + yi, shard)

    sibling = (dp, xi * CORES + 1 - ci)

    def send(src, dst, send_sem, recv_sem, to):
        pltpu.make_async_remote_copy(src_ref=src, dst_ref=dst, send_sem=send_sem, recv_sem=recv_sem,
                                     device_id=to, device_id_type=MESH).start()

    load_f = pltpu.make_async_copy(f_hbm, f, load_sem.at[8])
    load_f.start()

    def part_rows(i):
        q = (zi // 2 + 6 - i) % 4
        return q, pl.ds(pl.multiple_of(q * 96, 96), 96)

    def loads(i):
        _, rows = part_rows(i)
        return (pltpu.make_async_copy(g_hbm.at[rows], g.at[rows], load_sem.at[2 * i]),
                pltpu.make_async_copy(m_hbm.at[rows], m.at[rows], load_sem.at[2 * i + 1]))

    for i in range(4):
        for copy in loads(i):
            copy.start()

    barrier = pltpu.get_barrier_semaphore()

    def greet(k, _):
        pl.semaphore_signal(barrier, inc=1, device_id=plane_peer((dp + k) % DP), device_id_type=MESH)
        return 0
    lax.fori_loop(1, DP, greet, 0)
    for k in (1, 2, 3):
        pl.semaphore_signal(barrier, inc=1, device_id=x_peer(k), device_id_type=MESH)
    pl.semaphore_signal(barrier, inc=1, device_id=sibling, device_id_type=MESH)

    load_f.wait()
    for i in range(4):
        q, rows = part_rows(i)
        for copy in loads(i):
            copy.wait()
        value = (jnp.dot(g[rows, :], f[...], preferred_element_type=jnp.float32)
                 + jnp.dot(m[rows, :], f[...], preferred_element_type=jnp.float32))
        for j in range(8):
            part[q * 8 + j] = value[PIECE * j:PIECE * (j + 1)]
        if i == 0:
            pl.semaphore_wait(barrier, DP + 3)

        def scatter(j, _):
            to = q * 8 + j

            @pl.when(to != dp)
            def _():
                send(part.at[to], part_in.at[(to - dp + DP) % DP - 1], part_send, part_recv, plane_peer(to))
            return 0
        lax.fori_loop(0, 8, scatter, 0)

    def turn(i, _):
        lanes = pl.ds(pl.multiple_of(i * 128, 128), 128)
        gt[lanes, :] = g[:, lanes].T
        mt[lanes, :] = m[:, lanes].T
        return 0
    lax.fori_loop(0, BLOCKS, turn, 0)
    gt[D:, :] = jnp.zeros((PADDED - D, ROWS), jnp.bfloat16)
    mt[D:, :] = jnp.zeros((PADDED - D, ROWS), jnp.bfloat16)

    land(part_in, part_recv)
    total = part[dp]
    for k in range(DP - 1):
        total = total + part_in[k]
    span_all[dp] = total * (1.0 / DP)

    def spread(k, _):
        send(span_all.at[dp], span_all.at[dp], span_send, span_recv, plane_peer((dp + k) % DP))
        return 0
    lax.fori_loop(1, DP, spread, 0)
    land(span_all.at[pl.ds(0, DP - 1)], span_recv)

    for j in range(DP // 2):
        span[24 * j:24 * (j + 1), :] = jnp.concatenate([span_all[2 * j], span_all[2 * j + 1]], 0)
    high, low = split(span[...])
    span2[:, :RANK] = high
    span2[:, RANK:] = low

    gram[...] = lax.dot_general(span[...], span[...], (((0,), (0,)), ((), ())),
                                precision=lax.Precision.HIGHEST, preferred_element_type=jnp.float32)
    mine = pl.ds(pl.multiple_of(ci * 64, 64), 64)
    other = pl.ds(pl.multiple_of((1 - ci) * 64, 64), 64)
    send(gram.at[other], gram_in, gram_send.at[0], gram_recv.at[0], sibling)

    def product(start):
        rows = pl.ds(start, BIG)
        both = (jnp.dot(gt[rows, :], span2[...], preferred_element_type=jnp.float32)
                + jnp.dot(mt[rows, :], span2[...], preferred_element_type=jnp.float32))
        return both[:, :RANK] + both[:, RANK:]

    for i, k in enumerate(ORDER):
        start = pl.multiple_of((1 - ci) * HALF + ((b + k) % 4) * BIG, BIG)
        x[pl.ds(start, BIG), :] = product(start)
        send(x.at[pl.ds(start, BIG)], core_in.at[i], core_send, core_recv.at[i], sibling)
        if i == 0:
            land(gram_in, gram_recv.at[0])
            gram[mine, :] = gram[mine, :] + gram_in[...]
            for r in (1, 2, 3):
                send(gram.at[mine], gram_x.at[r - 1], gram_send.at[1], gram_recv.at[1], x_peer(r))

    for i, k in enumerate(ORDER):
        start = pl.multiple_of(ci * HALF + ((a + k) % 4) * BIG, BIG)
        value = product(start)
        land(core_in.at[i], core_recv.at[i])
        x[pl.ds(start, BIG), :] = value + core_in[i]
        if k:
            for j, kb in enumerate(ORDER):
                rows = pl.ds(pl.multiple_of(start + ((b + kb) % 4) * MID, MID), MID)
                send(x.at[rows], a_in.at[i, j], a_send, a_recv.at[i, j], a_peer(k))

    land(gram_x, gram_recv.at[1])
    land(gram_x, gram_send.at[1])
    gram[mine, :] = gram[mine, :] + gram_x[0] + gram_x[1] + gram_x[2]
    land(gram_in, gram_send.at[0])
    send(gram.at[mine], gram_back, gram_send.at[2], gram_recv.at[2], sibling)
    land(gram_back, gram_recv.at[2])
    lower[mine, :] = gram[mine, :]
    lower[other, :] = gram_back[...]
    row = lax.broadcasted_iota(jnp.int32, (RANK, RANK), 0)
    lane = lax.broadcasted_iota(jnp.int32, (RANK, RANK), 1)
    inverse[...] = (row == lane).astype(jnp.float32)

    def eliminate(first, last):
        def one(step, _):
            lower[...], inverse[...] = eight_columns(step, lower[...], inverse[...])
            return 0
        lax.fori_loop(first, last, one, 0)

    own = pl.multiple_of(ci * HALF + a * BIG, BIG)
    for j, kb in enumerate(ORDER):
        eliminate(2 * j, 2 * j + 2)
        rows = pl.ds(pl.multiple_of(own + ((b + kb) % 4) * MID, MID), MID)
        for i in range(3):
            land(a_in.at[i, j], a_recv.at[i, j])
        x[rows, :] = x[rows, :] + a_in[0, j] + a_in[1, j] + a_in[2, j]
        if kb:
            send(x.at[rows], b_in.at[j], b_send, b_recv.at[j], b_peer(kb))
    eliminate(8, 10)
    block = pl.multiple_of(own + b * MID, MID)
    rows = pl.ds(block, MID)
    for j in range(3):
        land(b_in.at[j], b_recv.at[j])
    x[rows, :] = x[rows, :] + b_in[0] + b_in[1] + b_in[2]
    for k in range(1, ZS):
        target = pl.ds(pl.multiple_of(block + ((zi + k) % ZS) * SMALL, SMALL), SMALL)
        send(x.at[target], z_in.at[k - 1], z_send, z_recv, z_peer(k))
    eliminate(10, 16)
    last = pl.ds(pl.multiple_of(block + zi * SMALL, SMALL), SMALL)
    land(z_in, z_recv)
    total = x[last, :]
    for k in range(ZS - 1):
        total = total + z_in[k]

    n_ref[last, :] = lax.dot_general(total * (1.0 / DP), inverse[...], (((1,), (1,)), ((), ())),
                                     precision=lax.Precision.HIGHEST, preferred_element_type=jnp.float32)
    for k in range(1, ZS):
        send(n_ref.at[last], n_ref.at[last], gz_send, gz_recv, z_peer(k))
    o_ref[...] = lax.dot_general(span[...], inverse[...], (((1,), (1,)), ((), ())),
                                 precision=lax.Precision.HIGHEST, preferred_element_type=jnp.float32)
    land(n_ref.at[pl.ds(0, (ZS - 1) * SMALL)], gz_recv)
    for j, kb in enumerate(ORDER[:3]):
        send(n_ref.at[rows], n_ref.at[rows], gb_send, gb_recv.at[j], b_peer(kb))
    for j, kb in enumerate((0, 2, 1, 3)):
        here = pl.ds(pl.multiple_of(own + ((b - kb + 4) % 4) * MID, MID), MID)
        if kb:
            land(n_ref.at[here], gb_recv.at[ORDER.index(kb)])
        for i, k in enumerate(ORDER[:3]):
            send(n_ref.at[here], n_ref.at[here], ga_send, ga_recv.at[i, j], a_peer(k))
        send(n_ref.at[here], n_ref.at[here], gc_send, gc_recv.at[0, j], sibling)
    for j, kb in enumerate((0, 2, 1, 3)):
        for i, k in enumerate(ORDER[:3]):
            there = pl.ds(pl.multiple_of(ci * HALF + ((a - k + 4) % 4) * BIG + ((b - kb + 4) % 4) * MID, MID), MID)
            land(n_ref.at[there], ga_recv.at[i, j])
            send(n_ref.at[there], n_ref.at[there], gc_send, gc_recv.at[i + 1, j], sibling)
    for i in range(4):
        for j in range(4):
            land(n_ref.at[pl.ds(0, MID)], gc_recv.at[i, j])

    land(part_in, part_send)
    land(part_in, span_send)
    land(gram_in, gram_send.at[2])
    land(x.at[pl.ds(0, HALF)], core_send)
    land(a_in, a_send)
    land(b_in, b_send)
    land(z_in, z_send)
    land(z_in, gz_send)
    land(b_in, gb_send)
    land(a_in, ga_send)
    land(x.at[pl.ds(0, HALF)], gc_send)


def exchange(g, m, f):
    dma = pltpu.SemaphoreType.DMA
    f32, bf16 = jnp.float32, jnp.bfloat16
    return pl.pallas_call(
        exchange_kernel,
        out_shape=(jax.ShapeDtypeStruct((PADDED, RANK), f32), jax.ShapeDtypeStruct((ROWS, RANK), f32)),
        in_specs=[pl.BlockSpec(memory_space=pl.ANY)] * 3,
        out_specs=(pl.BlockSpec(memory_space=pltpu.VMEM), pl.BlockSpec(memory_space=pltpu.VMEM)),
        scratch_shapes=[
            pltpu.VMEM((ROWS, D), bf16), pltpu.VMEM((ROWS, D), bf16), pltpu.VMEM((D, RANK), bf16),
            pltpu.VMEM((PADDED, ROWS), bf16), pltpu.VMEM((PADDED, ROWS), bf16),
            pltpu.VMEM((DP, PIECE, RANK), f32), pltpu.VMEM((DP - 1, PIECE, RANK), f32),
            pltpu.VMEM((DP, PIECE, RANK), f32), pltpu.VMEM((ROWS, RANK), f32), pltpu.VMEM((ROWS, 2 * RANK), bf16),
            pltpu.VMEM((RANK, RANK), f32), pltpu.VMEM((64, RANK), f32), pltpu.VMEM((3, 64, RANK), f32),
            pltpu.VMEM((64, RANK), f32),
            pltpu.VMEM((RANK, RANK), f32), pltpu.VMEM((RANK, RANK), f32),
            pltpu.VMEM((PADDED, RANK), f32), pltpu.VMEM((4, BIG, RANK), f32),
            pltpu.VMEM((3, 4, MID, RANK), f32), pltpu.VMEM((3, MID, RANK), f32),
            pltpu.VMEM((ZS - 1, SMALL, RANK), f32),
            dma((9,)), dma, dma, dma, dma, dma((3,)), dma((3,)), dma, dma((4,)), dma, dma((3, 4)), dma, dma((3,)),
            dma, dma, dma, dma, dma, dma((3,)), dma, dma((3, 4)), dma, dma((4, 4)),
        ],
        compiler_params=pltpu.CompilerParams(collective_id=0, has_side_effects=True, vmem_limit_bytes=VMEM_BYTES),
        cost_estimate=pl.CostEstimate(flops=4 * 10 ** 9, bytes_accessed=10 ** 7, transcendentals=0),
        name="exchange",
    )(g, m, f)


def residual_kernel(g_ref, m_ref, o_ref, n_ref, memory_ref, factor_ref, n_high, n_low):
    step = pl.program_id(0)

    @pl.when(step == 0)
    def _():
        high, low = split(n_ref[...])
        n_high[...] = high
        n_low[...] = low

    high, low = split(o_ref[...])

    def times(left, right):
        return lax.dot_general(left, right, (((1,), (1,)), ((), ())), preferred_element_type=jnp.float32)

    for start in range(0, D, 512):
        size = min(512, D - start)
        cols = pl.ds(start, size)
        update = (times(high, n_high[cols, :]) + times(high, n_low[cols, :])) + times(low, n_high[cols, :])
        corrected = g_ref[:, cols].astype(jnp.float32) + m_ref[:, cols].astype(jnp.float32)
        memory_ref[:, cols] = (corrected - update).astype(jnp.bfloat16)
    quarter = D // 4
    factor_ref[...] = n_ref[pl.ds(pl.multiple_of(step * quarter, quarter), quarter), :]


def residual(g, m, o, n):
    rows = ROWS // 4
    return pl.pallas_call(
        residual_kernel,
        grid=(4,),
        out_shape=(jax.ShapeDtypeStruct((ROWS, D), jnp.bfloat16), jax.ShapeDtypeStruct((D, RANK), jnp.float32)),
        in_specs=[
            pl.BlockSpec((rows, D), lambda i: (i, 0)), pl.BlockSpec((rows, D), lambda i: (i, 0)),
            pl.BlockSpec((rows, RANK), lambda i: (i, 0)), pl.BlockSpec((PADDED, RANK), lambda i: (0, 0)),
        ],
        out_specs=(pl.BlockSpec((rows, D), lambda i: (i, 0)), pl.BlockSpec((D // 4, RANK), lambda i: (i, 0))),
        scratch_shapes=[pltpu.VMEM((PADDED, RANK), jnp.bfloat16), pltpu.VMEM((PADDED, RANK), jnp.bfloat16)],
        compiler_params=pltpu.CompilerParams(vmem_limit_bytes=VMEM_BYTES),
        name="residual",
    )(g, m, o, n)


def per_device(gradient, memory, old_factor):
    g, m = gradient[0], memory[0]
    n, o = exchange(g, m, old_factor)
    new_memory, new_factor = residual(g, m, o, n)
    return (new_memory[None], new_factor)


def solution(mesh):
    in_specs = (P("dp", "shard", None), P("dp", "shard", None), P())
    out_specs = (P("dp", "shard", None), P())
    return jax.shard_map(
        per_device, mesh=mesh, in_specs=in_specs, out_specs=out_specs, check_vma=False
    )
```

```python
import functools

import jax
import jax.numpy as jnp
from jax import lax
from jax.experimental import pallas as pl
from jax.experimental.pallas import tpu as pltpu
from jax.sharding import PartitionSpec as P

MESH = pl.DeviceIdType.MESH
D = 3968
RANK = 128
ROWS = 384
ZS, YS, XS, CORES = 8, 4, 4, 2
DP = ZS * YS
PIECE = ROWS // DP
PADDED = 4096
HALF = PADDED // CORES
BIG = HALF // 4
MID = BIG // 4
SMALL = MID // ZS
BLOCKS = D // 128
FAR = (2, 1, 3, 0)
NEAR = (0, 1, 3, 2)
FAR_Z = (4, 3, 5, 2, 6, 1, 7, 0)
VMEM_BYTES = 48 * 1024 * 1024


def eight_columns(step, gram, inverse):
    row = lax.broadcasted_iota(jnp.int32, (RANK, 1), 0)
    row8 = lax.broadcasted_iota(jnp.int32, (8, RANK), 0)
    live = row[8:] + 8 * step < RANK
    columns = [jnp.broadcast_to(gram[:, k:k + 1], (RANK, RANK)) for k in range(8)]
    top = [column[:8] for column in columns]
    below = [jnp.where(live, column[8:], 0.0) for column in columns]
    gram8, inverse8 = gram[:8], inverse[:8]
    gram_rest, inverse_rest = gram[8:], inverse[8:]
    pivots = []
    for k in range(8):
        pivot = jnp.broadcast_to(top[k][k:k + 1], (8, RANK))
        reciprocal = 1.0 / pivot
        pivots.append(pivot[:1])
        factor8 = jnp.where(row8 > k, top[k] * reciprocal, 0.0)
        factor = below[k] * reciprocal[:1]
        for j in range(k + 1, 8):
            upper = top[j][k:k + 1]
            top[j] = top[j] - factor8 * upper
            below[j] = below[j] - factor * upper
        gram_row, inverse_row = gram8[k:k + 1], inverse8[k:k + 1]
        gram_rest = gram_rest - factor * gram_row
        inverse_rest = inverse_rest - factor * inverse_row
        gram8 = gram8 - factor8 * gram_row
        inverse8 = inverse8 - factor8 * inverse_row
    done = inverse8 * lax.rsqrt(jnp.concatenate(pivots, 0))
    inverse = jnp.concatenate([inverse_rest, done], 0)
    gram = jnp.concatenate([gram_rest, gram8], 0)
    return pltpu.roll(gram, RANK - 8, 1), inverse


def split(value):
    high = value.astype(jnp.bfloat16)
    return high, (value - high.astype(jnp.float32)).astype(jnp.bfloat16)


def land(ref, sem):
    pltpu.make_async_copy(ref, ref, sem).wait()


def exchange_kernel(g_hbm, m_hbm, f_hbm, new_ref, n_ref,
                    gm, f, gmt, part, part_in, span_all, span, span2, o2,
                    gram, gram_in, gram_x, gram_back, lower, inverse, x, core_in, a_in, z_in,
                    load_sem, part_send, part_recv, span_send, span_recv,
                    gram_send, gram_recv, core_send, core_recv, a_send, a_recv, z_send, z_recv,
                    gz_send, gz_recv, ga_send, ga_recv, gc_send, gc_recv):
    dp, shard = lax.axis_index("dp"), lax.axis_index("shard")
    zi, yi = dp // YS, dp % YS
    xi, ci = shard // CORES, shard % CORES
    a = xi * (1 - ci) + yi * ci
    b = yi * (1 - ci) + xi * ci

    def plane_peer(j):
        return (j, shard)

    def a_peer(k):
        return (zi * YS + (yi + k * ci) % 4, ((xi + k * (1 - ci)) % 4) * CORES + ci)

    def bz_peer(kb, kz):
        return (((zi + kz) % ZS) * YS + (yi + kb * (1 - ci)) % 4, ((xi + kb * ci) % 4) * CORES + ci)

    def xz_peer(kx, kz):
        return (((zi + kz) % ZS) * YS + yi, ((xi + kx) % 4) * CORES + ci)

    sibling = (dp, xi * CORES + 1 - ci)

    def send(src, dst, send_sem, recv_sem, to):
        pltpu.make_async_remote_copy(src_ref=src, dst_ref=dst, send_sem=send_sem, recv_sem=recv_sem,
                                     device_id=to, device_id_type=MESH).start()

    def greet(to):
        pl.semaphore_signal(barrier, inc=1, device_id=to, device_id_type=MESH)

    load_f = pltpu.make_async_copy(f_hbm, f, load_sem.at[8])
    load_f.start()

    def quarter(i):
        return (zi // 2 + 6 - i) % 4

    def loads(i):
        q = quarter(i)
        rows = pl.ds(pl.multiple_of(q * 96, 96), 96)
        first = pl.ds(pl.multiple_of(q * 192, 96), 96)
        second = pl.ds(pl.multiple_of(q * 192 + 96, 96), 96)
        return (pltpu.make_async_copy(g_hbm.at[rows], gm.at[first], load_sem.at[2 * i]),
                pltpu.make_async_copy(m_hbm.at[rows], gm.at[second], load_sem.at[2 * i + 1]))

    for i in range(4):
        for copy in loads(i):
            copy.start()

    barrier = pltpu.get_barrier_semaphore()

    def greet_plane(k, _):
        greet(plane_peer((dp + k) % DP))
        return 0
    lax.fori_loop(1, DP, greet_plane, 0)

    def greet_x(k, _):
        for kx in (1, 2, 3):
            greet(xz_peer(kx, k))
        return 0
    lax.fori_loop(0, 1 + (ZS - 1) * ci, greet_x, 0)
    greet(sibling)

    load_f.wait()
    for i in range(4):
        q = quarter(i)
        for copy in loads(i):
            copy.wait()
        both = jnp.dot(gm[pl.ds(pl.multiple_of(q * 192, 192), 192), :], f[...], preferred_element_type=jnp.float32)
        value = both[:96] + both[96:]
        for j in range(8):
            part[q * 8 + j] = value[PIECE * j:PIECE * (j + 1)]
        if i == 0:
            pl.semaphore_wait(barrier, DP + 3 + 3 * (ZS - 1) * ci)

        def scatter(j, _):
            to = q * 8 + j

            @pl.when(to != dp)
            def _():
                send(part.at[to], part_in.at[(to - dp + DP) % DP - 1], part_send, part_recv, plane_peer(to))
            return 0
        lax.fori_loop(0, 8, scatter, 0)

    def turn(i, _):
        lanes = pl.ds(pl.multiple_of(i * 128, 128), 128)
        gmt[lanes, :] = gm[:, lanes].T
        return 0
    lax.fori_loop(0, BLOCKS, turn, 0)
    gmt[D:, :] = jnp.zeros((PADDED - D, 2 * ROWS), jnp.bfloat16)

    land(part_in, part_recv)
    total = part[dp]
    for k in range(DP - 1):
        total = total + part_in[k]
    span_all[dp] = total * (1.0 / DP)

    def spread(k, _):
        send(span_all.at[dp], span_all.at[dp], span_send, span_recv, plane_peer((dp + k) % DP))
        return 0
    lax.fori_loop(1, DP, spread, 0)
    land(span_all.at[pl.ds(0, DP - 1)], span_recv)

    for j in range(DP // 2):
        span[24 * j:24 * (j + 1), :] = jnp.concatenate([span_all[2 * j], span_all[2 * j + 1]], 0)
    for q in range(4):
        high, low = split(span[96 * q:96 * (q + 1), :])
        for start in (192 * q, 192 * q + 96):
            span2[start:start + 96, :RANK] = high
            span2[start:start + 96, RANK:] = low

    mine = pl.ds(pl.multiple_of(ci * 64, 64), 64)
    other = pl.ds(pl.multiple_of((1 - ci) * 64, 64), 64)

    def product(start):
        both = jnp.dot(gmt[pl.ds(start, BIG), :], span2[...], preferred_element_type=jnp.float32)
        return both[:, :RANK] + both[:, RANK:]

    def for_sibling(i):
        start = pl.multiple_of((1 - ci) * HALF + ((b + FAR[i]) % 4) * BIG, BIG)
        x[pl.ds(start, BIG), :] = product(start)
        send(x.at[pl.ds(start, BIG)], core_in.at[i], core_send, core_recv.at[i], sibling)

    def for_axis(i):
        start = pl.multiple_of(ci * HALF + ((a + FAR[i]) % 4) * BIG, BIG)
        value = product(start)
        land(core_in.at[i], core_recv.at[i])
        x[pl.ds(start, BIG), :] = value + core_in[i]
        if FAR[i]:
            for j, kb in enumerate(FAR):
                rows = pl.ds(pl.multiple_of(start + ((b + kb) % 4) * MID, MID), MID)
                send(x.at[rows], a_in.at[i, j], a_send, a_recv.at[i, j], a_peer(FAR[i]))

    for_sibling(0)
    gram[...] = lax.dot_general(span[...], span[...], (((0,), (0,)), ((), ())),
                                precision=lax.Precision.HIGHEST, preferred_element_type=jnp.float32)
    send(gram.at[other], gram_in, gram_send.at[0], gram_recv.at[0], sibling)
    for_sibling(1)
    for_axis(0)
    land(gram_in, gram_recv.at[0])
    gram[mine, :] = gram[mine, :] + gram_in[...]
    for r in (1, 2, 3):
        send(gram.at[mine], gram_x.at[r - 1], gram_send.at[1], gram_recv.at[1], xz_peer(r, 0))
    for_sibling(2)
    for_axis(1)
    for_sibling(3)
    for_axis(2)
    for_axis(3)

    land(gram_x, gram_recv.at[1])
    land(gram_x, gram_send.at[1])
    gram[mine, :] = gram[mine, :] + gram_x[0] + gram_x[1] + gram_x[2]
    send(gram.at[mine], gram_back, gram_send.at[2], gram_recv.at[2], sibling)
    lower[mine, :] = gram[mine, :]
    row = lax.broadcasted_iota(jnp.int32, (RANK, RANK), 0)
    lane = lax.broadcasted_iota(jnp.int32, (RANK, RANK), 1)
    inverse[...] = (row == lane).astype(jnp.float32)

    def eliminate(first, last):
        def one(step, _):
            lower[...], inverse[...] = eight_columns(step, lower[...], inverse[...])
            return 0
        lax.fori_loop(first, last, one, 0)

    own = pl.multiple_of(ci * HALF + a * BIG, BIG)
    for j, kb in enumerate(FAR):
        block = pl.multiple_of(own + ((b + kb) % 4) * MID, MID)
        rows = pl.ds(block, MID)
        for i in range(3):
            land(a_in.at[i, j], a_recv.at[i, j])
        x[rows, :] = x[rows, :] + a_in[0, j] + a_in[1, j] + a_in[2, j]
        for kz in FAR_Z:
            if kb or kz:
                piece = pl.ds(pl.multiple_of(block + ((zi + kz) % ZS) * SMALL, SMALL), SMALL)
                slot = ZS * j + kz - (1 if kb == 0 else 0)
                send(x.at[piece], z_in.at[slot], z_send, z_recv, bz_peer(kb, kz))
        if j == 0:
            land(gram_back, gram_recv.at[2])
            lower[other, :] = gram_back[...]
        eliminate(2 * j, 2 * j + 2)
    eliminate(8, 16)
    span_in_basis = lax.dot_general(span[...], inverse[...], (((1,), (1,)), ((), ())),
                                    precision=lax.Precision.HIGHEST, preferred_element_type=jnp.float32)
    high, low = split(span_in_basis)
    o2[:, :RANK] = high
    o2[:, RANK:] = low
    last = pl.ds(pl.multiple_of(own + b * MID + zi * SMALL, SMALL), SMALL)
    land(z_in, z_recv)
    total = x[last, :]
    for k in range(4 * ZS - 1):
        total = total + z_in[k]

    n_ref[last, :] = lax.dot_general(total * (1.0 / DP), inverse[...], (((1,), (1,)), ((), ())),
                                     precision=lax.Precision.HIGHEST, preferred_element_type=jnp.float32)
    for j, kb in enumerate(NEAR):
        for kz in FAR_Z:
            if kb or kz:
                send(n_ref.at[last], n_ref.at[last], gz_send, gz_recv.at[j], bz_peer(kb, kz))

    def block_of(core, first, second):
        return pl.multiple_of(core * HALF + first * BIG + second * MID, MID)

    def residual(start):
        @pl.when(start < D)
        def _():
            cols = pl.ds(start, MID)
            high, low = split(n_ref[cols, :])
            update = (lax.dot_general(o2[...], jnp.concatenate([high, high], 1), (((1,), (1,)), ((), ())),
                                      preferred_element_type=jnp.float32)
                      + lax.dot_general(o2[:, :RANK], low, (((1,), (1,)), ((), ())),
                                        preferred_element_type=jnp.float32))
            for q in range(4):
                corrected = (gm[192 * q:192 * q + 96, cols].astype(jnp.float32)
                             + gm[192 * q + 96:192 * q + 192, cols].astype(jnp.float32))
                new_ref[96 * q:96 * (q + 1), cols] = (corrected - update[96 * q:96 * (q + 1)]).astype(jnp.bfloat16)

    arrivals = [(i, j) for i in (3,) for j in range(4)] + [(i, j) for j in range(4) for i in range(3)]

    def take_own(i, j):
        if i == 3:
            start = block_of(ci, a, (b - NEAR[j] + 4) % 4)
            here = pl.ds(start, MID)
            land(n_ref.at[pl.ds(0, (ZS - 1) * SMALL if NEAR[j] == 0 else MID)], gz_recv.at[j])
            for r in range(3):
                send(n_ref.at[here], n_ref.at[here], ga_send, ga_recv.at[r, j], a_peer(FAR[r]))
        else:
            start = block_of(ci, (a - FAR[i] + 4) % 4, (b - NEAR[j] + 4) % 4)
            here = pl.ds(start, MID)
            land(n_ref.at[here], ga_recv.at[i, j])
        send(n_ref.at[here], n_ref.at[here], gc_send, gc_recv.at[i, j], sibling)
        return start

    def take_sibling(i, j):
        start = block_of(1 - ci, (b - FAR[i] + 4) % 4, (a - NEAR[j] + 4) % 4)
        land(n_ref.at[pl.ds(start, MID)], gc_recv.at[i, j])
        residual(start)

    for n, (i, j) in enumerate(arrivals):
        start = take_own(i, j)
        residual(start)
        if n >= 4:
            take_sibling(*arrivals[n - 4])
    for i, j in arrivals[-4:]:
        take_sibling(i, j)

    land(part_in, part_send)
    land(part_in, span_send)
    land(gram_in, gram_send.at[0])
    land(gram_in, gram_send.at[2])
    land(x.at[pl.ds(0, HALF)], core_send)
    land(a_in, a_send)
    land(z_in, z_send)
    land(z_in, gz_send)
    land(a_in, ga_send)
    land(x.at[pl.ds(0, HALF)], gc_send)


def exchange(g, m, f):
    dma = pltpu.SemaphoreType.DMA
    f32, bf16 = jnp.float32, jnp.bfloat16
    return pl.pallas_call(
        exchange_kernel,
        out_shape=(jax.ShapeDtypeStruct((ROWS, D), bf16), jax.ShapeDtypeStruct((PADDED, RANK), f32)),
        in_specs=[pl.BlockSpec(memory_space=pltpu.HBM)] * 3,
        out_specs=(pl.BlockSpec(memory_space=pltpu.VMEM), pl.BlockSpec(memory_space=pltpu.VMEM)),
        scratch_shapes=[
            pltpu.VMEM((2 * ROWS, D), bf16), pltpu.VMEM((D, RANK), bf16), pltpu.VMEM((PADDED, 2 * ROWS), bf16),
            pltpu.VMEM((DP, PIECE, RANK), f32), pltpu.VMEM((DP - 1, PIECE, RANK), f32),
            pltpu.VMEM((DP, PIECE, RANK), f32), pltpu.VMEM((ROWS, RANK), f32),
            pltpu.VMEM((2 * ROWS, 2 * RANK), bf16), pltpu.VMEM((ROWS, 2 * RANK), bf16),
            pltpu.VMEM((RANK, RANK), f32), pltpu.VMEM((64, RANK), f32), pltpu.VMEM((3, 64, RANK), f32),
            pltpu.VMEM((64, RANK), f32), pltpu.VMEM((RANK, RANK), f32), pltpu.VMEM((RANK, RANK), f32),
            pltpu.VMEM((PADDED, RANK), f32), pltpu.VMEM((4, BIG, RANK), f32),
            pltpu.VMEM((3, 4, MID, RANK), f32), pltpu.VMEM((4 * ZS - 1, SMALL, RANK), f32),
            dma((9,)), dma, dma, dma, dma, dma((3,)), dma((3,)), dma, dma((4,)), dma, dma((3, 4)), dma, dma,
            dma, dma((4,)), dma, dma((3, 4)), dma, dma((4, 4)),
        ],
        compiler_params=pltpu.CompilerParams(collective_id=0, has_side_effects=True, vmem_limit_bytes=VMEM_BYTES),
        cost_estimate=pl.CostEstimate(flops=4 * 10 ** 9, bytes_accessed=10 ** 7, transcendentals=0),
        name="exchange",
    )(g, m, f)


def per_device(gradient, memory, old_factor):
    new_memory, new_factor = exchange(gradient[0], memory[0], old_factor)
    return (new_memory[None], new_factor[:D])


def solution(mesh):
    in_specs = (P("dp", "shard", None), P("dp", "shard", None), P())
    out_specs = (P("dp", "shard", None), P())
    return jax.shard_map(
        per_device, mesh=mesh, in_specs=in_specs, out_specs=out_specs, check_vma=False
    )
```

```python
import functools

import jax
import jax.numpy as jnp
from jax import lax
from jax.experimental import pallas as pl
from jax.experimental.pallas import tpu as pltpu
from jax.sharding import PartitionSpec as P

MESH = pl.DeviceIdType.MESH
D = 3968
RANK = 128
ROWS = 384
ZS, YS, XS, CORES = 8, 4, 4, 2
DP = ZS * YS
PIECE = ROWS // DP
PADDED = 4096
HALF = PADDED // CORES
BIG = HALF // 4
MID = BIG // 4
SMALL = MID // ZS
BLOCKS = D // 128
FAR = (2, 1, 3, 0)
NEAR = (0, 1, 3, 2)
FAR_Z = (4, 3, 5, 2, 6, 1, 7, 0)
VMEM_BYTES = 48 * 1024 * 1024
STORE_VMEM = 16 * 1024 * 1024


def eight_columns(live_from, gram, inverse):
    size = gram.shape[0]
    row = lax.broadcasted_iota(jnp.int32, (size, 1), 0)
    row8 = lax.broadcasted_iota(jnp.int32, (8, RANK), 0)
    live = row[8:] < live_from
    columns = [jnp.broadcast_to(gram[:, k:k + 1], (size, RANK)) for k in range(8)]
    top = [column[:8] for column in columns]
    below = [jnp.where(live, column[8:], 0.0) for column in columns]
    gram8, inverse8 = gram[:8], inverse[:8]
    gram_rest, inverse_rest = gram[8:], inverse[8:]
    pivots = []
    for k in range(8):
        pivot = jnp.broadcast_to(top[k][k:k + 1], (8, RANK))
        reciprocal = 1.0 / pivot
        pivots.append(pivot[:1])
        factor8 = jnp.where(row8 > k, top[k] * reciprocal, 0.0)
        factor = below[k] * reciprocal[:1]
        for j in range(k + 1, 8):
            upper = top[j][k:k + 1]
            top[j] = top[j] - factor8 * upper
            below[j] = below[j] - factor * upper
        gram_row, inverse_row = gram8[k:k + 1], inverse8[k:k + 1]
        gram_rest = gram_rest - factor * gram_row
        inverse_rest = inverse_rest - factor * inverse_row
        gram8 = gram8 - factor8 * gram_row
        inverse8 = inverse8 - factor8 * inverse_row
    done = inverse8 * lax.rsqrt(jnp.concatenate(pivots, 0))
    gram = pltpu.roll(jnp.concatenate([gram_rest, gram8], 0), RANK - 8, 1)
    return gram, jnp.concatenate([inverse_rest, inverse8], 0), done


def split(value):
    high = value.astype(jnp.bfloat16)
    return high, (value - high.astype(jnp.float32)).astype(jnp.bfloat16)


def land(ref, sem):
    pltpu.make_async_copy(ref, ref, sem).wait()


def exchange_kernel(g_hbm, m_hbm, f, new_ref, n_ref,
                    gm, gmt, part, part_y, part_z, span_all, span, span2, o2,
                    gram, gram_in, gram_x, gram_back, lower, work, inverse, x, core_in, a_in, z_in,
                    load_sem, party_send, party_recv, part_send, part_recv, span_send, span_recv,
                    gram_send, gram_recv, core_send, core_recv, a_send, a_recv, z_send, z_recv,
                    gz_send, gz_recv, ga_send, ga_recv, gc_send, gc_recv):
    dp, shard = lax.axis_index("dp"), lax.axis_index("shard")
    zi, yi = dp // YS, dp % YS
    xi, ci = shard // CORES, shard % CORES
    a = xi * (1 - ci) + yi * ci
    b = yi * (1 - ci) + xi * ci

    def plane_peer(j):
        return (j, shard)

    def a_peer(k):
        return (zi * YS + (yi + k * ci) % 4, ((xi + k * (1 - ci)) % 4) * CORES + ci)

    def y_peer(k):
        return (zi * YS + (yi + k) % YS, shard)

    def bz_peer(kb, kz):
        return (((zi + kz) % ZS) * YS + (yi + kb * (1 - ci)) % 4, ((xi + kb * ci) % 4) * CORES + ci)

    def xz_peer(kx, kz):
        return (((zi + kz) % ZS) * YS + yi, ((xi + kx) % 4) * CORES + ci)

    sibling = (dp, xi * CORES + 1 - ci)

    def send(src, dst, send_sem, recv_sem, to):
        pltpu.make_async_remote_copy(src_ref=src, dst_ref=dst, send_sem=send_sem, recv_sem=recv_sem,
                                     device_id=to, device_id_type=MESH).start()

    def greet(to):
        pl.semaphore_signal(barrier, inc=1, device_id=to, device_id_type=MESH)


    def quarter(i):
        return (yi + FAR[i]) % 4

    def loads(i):
        q = quarter(i)
        rows = pl.ds(pl.multiple_of(q * 96, 96), 96)
        first = pl.ds(pl.multiple_of(q * 192, 96), 96)
        second = pl.ds(pl.multiple_of(q * 192 + 96, 96), 96)
        return (pltpu.make_async_copy(g_hbm.at[rows], gm.at[first], load_sem.at[2 * i]),
                pltpu.make_async_copy(m_hbm.at[rows], gm.at[second], load_sem.at[2 * i + 1]))

    for i in range(4):
        for copy in loads(i):
            copy.start()

    barrier = pltpu.get_barrier_semaphore()
    for k in (4, 3, 5, 2, 6, 1, 7):
        greet(xz_peer(0, k))
    for k in (2, 1, 3):
        greet(y_peer(k))
        greet(xz_peer(k, 0))
    greet(sibling)

    for i in range(4):
        q = quarter(i)
        for copy in loads(i):
            copy.wait()
        both = jnp.dot(gm[pl.ds(pl.multiple_of(q * 192, 192), 192), :], f[:D, :], preferred_element_type=jnp.float32)
        value = both[:96] + both[96:]
        for j in range(ZS):
            part[q * ZS + j] = value[PIECE * j:PIECE * (j + 1)]
        if i == 0:
            pl.semaphore_wait(barrier, 14)
        if FAR[i]:
            send(part.at[pl.ds(q * ZS, ZS)], part_y.at[i], party_send, party_recv.at[i], y_peer(FAR[i]))

    def turn(i, _):
        lanes = pl.ds(pl.multiple_of(i * 128, 128), 128)
        gmt[lanes, :] = gm[:, lanes].T
        return 0
    lax.fori_loop(0, BLOCKS // 2, turn, 0)
    for i in range(3):
        land(part_y.at[i], party_recv.at[i])
    for j in range(ZS):
        to = (zi + FAR_Z[j]) % ZS
        slot = yi * ZS + to
        part[slot] = (part[slot] + part_y[0, to]) + (part_y[1, to] + part_y[2, to])
        if FAR_Z[j]:
            send(part.at[slot], part_z.at[FAR_Z[j] - 1], part_send, part_recv, xz_peer(0, FAR_Z[j]))
    lax.fori_loop(BLOCKS // 2, BLOCKS, turn, 0)
    gmt[D:, :] = jnp.zeros((PADDED - D, 2 * ROWS), jnp.bfloat16)

    me = yi * ZS + zi
    land(part_z, part_recv)
    total = part[me]
    for k in range(ZS - 1):
        total = total + part_z[k]
    span_all[me] = total * (1.0 / DP)

    def spread(k, _):
        send(span_all.at[me], span_all.at[me], span_send, span_recv, plane_peer((dp + k) % DP))
        return 0
    lax.fori_loop(10, 23, spread, 0)
    lax.fori_loop(1, 10, spread, 0)
    lax.fori_loop(23, DP, spread, 0)
    land(span_all.at[pl.ds(0, DP - 1)], span_recv)

    for j in range(DP // 2):
        span[24 * j:24 * (j + 1), :] = jnp.concatenate([span_all[2 * j], span_all[2 * j + 1]], 0)
    for q in range(4):
        high, low = split(span[96 * q:96 * (q + 1), :])
        for start in (192 * q, 192 * q + 96):
            span2[start:start + 96, :RANK] = high
            span2[start:start + 96, RANK:] = low

    mine = pl.ds(pl.multiple_of(ci * 64, 64), 64)
    other = pl.ds(pl.multiple_of((1 - ci) * 64, 64), 64)

    def product(start):
        both = jnp.dot(gmt[pl.ds(start, BIG), :], span2[...], preferred_element_type=jnp.float32)
        return both[:, :RANK] + both[:, RANK:]

    def for_sibling(i):
        start = pl.multiple_of((1 - ci) * HALF + ((b + FAR[i]) % 4) * BIG, BIG)
        x[pl.ds(start, BIG), :] = product(start)
        send(x.at[pl.ds(start, BIG)], core_in.at[i], core_send, core_recv.at[i], sibling)

    def for_axis(i):
        start = pl.multiple_of(ci * HALF + ((a + FAR[i]) % 4) * BIG, BIG)
        value = product(start)
        land(core_in.at[i], core_recv.at[i])
        x[pl.ds(start, BIG), :] = value + core_in[i]
        if FAR[i]:
            for j, kb in enumerate(FAR):
                rows = pl.ds(pl.multiple_of(start + ((b + kb) % 4) * MID, MID), MID)
                send(x.at[rows], a_in.at[i, j], a_send, a_recv.at[i, j], a_peer(FAR[i]))

    gram[...] = lax.dot_general(span[...], span[...], (((0,), (0,)), ((), ())),
                                precision=lax.Precision.HIGHEST, preferred_element_type=jnp.float32)
    send(gram.at[other], gram_in, gram_send.at[0], gram_recv.at[0], sibling)
    for_sibling(0)
    for_sibling(1)
    land(gram_in, gram_recv.at[0])
    gram[mine, :] = gram[mine, :] + gram_in[...]
    for r in (1, 2, 3):
        send(gram.at[mine], gram_x.at[r - 1], gram_send.at[1], gram_recv.at[1], xz_peer(r, 0))
    for_axis(0)
    for_sibling(2)
    for_axis(1)
    for_sibling(3)
    for_axis(2)
    for_axis(3)
    row = lax.broadcasted_iota(jnp.int32, (RANK, RANK), 0)
    lane = lax.broadcasted_iota(jnp.int32, (RANK, RANK), 1)
    work[...] = (row == lane).astype(jnp.float32)

    def eliminate(first, last):
        size = RANK - 32 * (first // 4)

        def one(step, _):
            rows = pl.ds(pl.multiple_of(step * 8, 8), 8)
            lower[:size, :], work[:size, :], inverse[rows, :] = eight_columns(
                RANK - 8 * step, lower[:size, :], work[:size, :])
            return 0
        lax.fori_loop(first, last, one, 0)

    own = pl.multiple_of(ci * HALF + a * BIG, BIG)
    for j, kb in enumerate(FAR):
        block = pl.multiple_of(own + ((b + kb) % 4) * MID, MID)
        rows = pl.ds(block, MID)
        for i in range(3):
            land(a_in.at[i, j], a_recv.at[i, j])
        x[rows, :] = x[rows, :] + a_in[0, j] + a_in[1, j] + a_in[2, j]
        for kz in FAR_Z:
            if kb or kz:
                piece = pl.ds(pl.multiple_of(block + ((zi + kz) % ZS) * SMALL, SMALL), SMALL)
                slot = ZS * j + kz - (1 if kb == 0 else 0)
                send(x.at[piece], z_in.at[slot], z_send, z_recv, bz_peer(kb, kz))
        if j == 0:
            land(gram_x, gram_recv.at[1])
            land(gram_x, gram_send.at[1])
            gram[mine, :] = gram[mine, :] + gram_x[0] + gram_x[1] + gram_x[2]
            send(gram.at[mine], gram_back, gram_send.at[2], gram_recv.at[2], sibling)
            lower[mine, :] = gram[mine, :]
        if j == 1:
            land(gram_back, gram_recv.at[2])
            lower[other, :] = gram_back[...]
            eliminate(0, 1)
        if j == 2:
            eliminate(1, 3)
    eliminate(3, 4)
    eliminate(4, 8)
    eliminate(8, 12)
    eliminate(12, 16)
    span_in_basis = lax.dot_general(span[...], inverse[...], (((1,), (1,)), ((), ())),
                                    precision=lax.Precision.HIGHEST, preferred_element_type=jnp.float32)
    high, low = split(span_in_basis)
    o2[:, :RANK] = high
    o2[:, RANK:] = low
    last = pl.ds(pl.multiple_of(own + b * MID + zi * SMALL, SMALL), SMALL)
    land(z_in, z_recv)
    total = x[last, :]
    for k in range(4 * ZS - 1):
        total = total + z_in[k]

    n_ref[last, :] = lax.dot_general(total * (1.0 / DP), inverse[...], (((1,), (1,)), ((), ())),
                                     precision=lax.Precision.HIGHEST, preferred_element_type=jnp.float32)
    for j, kb in enumerate(NEAR):
        for kz in FAR_Z:
            if kb or kz:
                send(n_ref.at[last], n_ref.at[last], gz_send, gz_recv.at[j], bz_peer(kb, kz))

    def block_of(core, first, second):
        return pl.multiple_of(core * HALF + first * BIG + second * MID, MID)

    def residual(start):
        @pl.when(start < D)
        def _():
            cols = pl.ds(start, MID)
            high, low = split(n_ref[cols, :])
            update = (lax.dot_general(o2[...], jnp.concatenate([high, high], 1), (((1,), (1,)), ((), ())),
                                      preferred_element_type=jnp.float32)
                      + lax.dot_general(o2[:, :RANK], low, (((1,), (1,)), ((), ())),
                                        preferred_element_type=jnp.float32))
            for q in range(4):
                corrected = (gm[192 * q:192 * q + 96, cols].astype(jnp.float32)
                             + gm[192 * q + 96:192 * q + 192, cols].astype(jnp.float32))
                new_ref[96 * q:96 * (q + 1), cols] = (corrected - update[96 * q:96 * (q + 1)]).astype(jnp.bfloat16)

    arrivals = [(i, j) for i in (3,) for j in range(4)] + [(i, j) for j in range(4) for i in range(3)]

    def take_own(i, j):
        if i == 3:
            start = block_of(ci, a, (b - NEAR[j] + 4) % 4)
            here = pl.ds(start, MID)
            land(n_ref.at[pl.ds(0, (ZS - 1) * SMALL if NEAR[j] == 0 else MID)], gz_recv.at[j])
            for r in range(3):
                send(n_ref.at[here], n_ref.at[here], ga_send, ga_recv.at[r, j], a_peer(FAR[r]))
        else:
            start = block_of(ci, (a - FAR[i] + 4) % 4, (b - NEAR[j] + 4) % 4)
            here = pl.ds(start, MID)
            land(n_ref.at[here], ga_recv.at[i, j])
        send(n_ref.at[here], n_ref.at[here], gc_send, gc_recv.at[i, j], sibling)
        return start

    def take_sibling(i, j):
        start = block_of(1 - ci, (b - FAR[i] + 4) % 4, (a - NEAR[j] + 4) % 4)
        land(n_ref.at[pl.ds(start, MID)], gc_recv.at[i, j])
        residual(start)

    for n, (i, j) in enumerate(arrivals):
        start = take_own(i, j)
        residual(start)
        if n >= 4:
            take_sibling(*arrivals[n - 4])
    for i, j in arrivals[-4:]:
        take_sibling(i, j)

    land(part_y, party_send)
    land(part_z, part_send)
    land(span_all.at[pl.ds(0, DP - 1)], span_send)
    land(gram_in, gram_send.at[0])
    land(gram_in, gram_send.at[2])
    land(x.at[pl.ds(0, HALF)], core_send)
    land(a_in, a_send)
    land(z_in, z_send)
    land(z_in, gz_send)
    land(a_in, ga_send)
    land(x.at[pl.ds(0, HALF)], gc_send)


def exchange(g, m, f):
    dma = pltpu.SemaphoreType.DMA
    f32, bf16 = jnp.float32, jnp.bfloat16
    return pl.pallas_call(
        exchange_kernel,
        out_shape=(jax.ShapeDtypeStruct((ROWS, D), bf16), jax.ShapeDtypeStruct((PADDED, RANK), f32)),
        in_specs=[pl.BlockSpec(memory_space=pltpu.HBM)] * 2 + [pl.BlockSpec(memory_space=pltpu.VMEM)],
        out_specs=(pl.BlockSpec(memory_space=pltpu.VMEM), pl.BlockSpec(memory_space=pltpu.VMEM)),
        scratch_shapes=[
            pltpu.VMEM((2 * ROWS, D), bf16), pltpu.VMEM((PADDED, 2 * ROWS), bf16),
            pltpu.VMEM((DP, PIECE, RANK), f32), pltpu.VMEM((3, ZS, PIECE, RANK), f32),
            pltpu.VMEM((ZS - 1, PIECE, RANK), f32),
            pltpu.VMEM((DP, PIECE, RANK), f32), pltpu.VMEM((ROWS, RANK), f32),
            pltpu.VMEM((2 * ROWS, 2 * RANK), bf16), pltpu.VMEM((ROWS, 2 * RANK), bf16),
            pltpu.VMEM((RANK, RANK), f32), pltpu.VMEM((64, RANK), f32), pltpu.VMEM((3, 64, RANK), f32),
            pltpu.VMEM((64, RANK), f32), pltpu.VMEM((RANK, RANK), f32), pltpu.VMEM((RANK, RANK), f32),
            pltpu.VMEM((RANK, RANK), f32),
            pltpu.VMEM((PADDED, RANK), f32), pltpu.VMEM((4, BIG, RANK), f32),
            pltpu.VMEM((3, 4, MID, RANK), f32), pltpu.VMEM((4 * ZS - 1, SMALL, RANK), f32),
            dma((8,)), dma, dma((3,)), dma, dma, dma, dma, dma((3,)), dma((3,)), dma, dma((4,)), dma, dma((3, 4)), dma, dma,
            dma, dma((4,)), dma, dma((3, 4)), dma, dma((4, 4)),
        ],
        compiler_params=pltpu.CompilerParams(collective_id=0, has_side_effects=True, vmem_limit_bytes=VMEM_BYTES),
        cost_estimate=pl.CostEstimate(flops=4 * 10 ** 9, bytes_accessed=10 ** 7, transcendentals=0),
        name="exchange",
    )(g, m, f)


def store_kernel(new_ref, n_ref, memory_ref, factor_ref, sems):
    copies = [pltpu.make_async_copy(new_ref.at[pl.ds(96 * i, 96)], memory_ref.at[pl.ds(96 * i, 96)], sems.at[i])
              for i in range(4)]
    quarter = D // 4
    copies += [pltpu.make_async_copy(n_ref.at[pl.ds(quarter * i, quarter)], factor_ref.at[pl.ds(quarter * i, quarter)],
                                     sems.at[4 + i]) for i in range(4)]
    for copy in copies:
        copy.start()
    for copy in copies:
        copy.wait()


def store(new, n):
    return pl.pallas_call(
        store_kernel,
        out_shape=(jax.ShapeDtypeStruct((ROWS, D), jnp.bfloat16), jax.ShapeDtypeStruct((D, RANK), jnp.float32)),
        in_specs=[pl.BlockSpec(memory_space=pltpu.VMEM)] * 2,
        out_specs=(pl.BlockSpec(memory_space=pltpu.HBM), pl.BlockSpec(memory_space=pltpu.HBM)),
        scratch_shapes=[pltpu.SemaphoreType.DMA((8,))],
        compiler_params=pltpu.CompilerParams(vmem_limit_bytes=STORE_VMEM),
        name="store",
    )(new, n)


def per_device(gradient, memory, old_factor):
    new_memory, new_factor = store(*exchange(gradient[0], memory[0], old_factor))
    return (new_memory[None], new_factor)


def solution(mesh):
    in_specs = (P("dp", "shard", None), P("dp", "shard", None), P())
    out_specs = (P("dp", "shard", None), P())
    return jax.shard_map(
        per_device, mesh=mesh, in_specs=in_specs, out_specs=out_specs, check_vma=False
    )
```

```python
import functools

import jax
import jax.numpy as jnp
from jax import lax
from jax.experimental import pallas as pl
from jax.experimental.pallas import tpu as pltpu
from jax.sharding import PartitionSpec as P

MESH = pl.DeviceIdType.MESH
D = 3968
RANK = 128
ROWS = 384
ZS, YS, XS, CORES = 8, 4, 4, 2
DP = ZS * YS
PIECE = ROWS // DP
PADDED = 4096
HALF = PADDED // CORES
BIG = HALF // 4
HALF_BIG = BIG // 2
PAIR = HALF_BIG // 2
GROUP = PAIR // 2
SMALL = GROUP // ZS
BLOCKS = D // 128
FAR = (2, 1, 3, 0)
FAR_Z = (4, 3, 5, 2, 6, 1, 7, 0)
VMEM_BYTES = 48 * 1024 * 1024
STORE_VMEM = 16 * 1024 * 1024


def eight_columns(live_from, gram, inverse):
    size = gram.shape[0]
    row = lax.broadcasted_iota(jnp.int32, (size, 1), 0)
    row8 = lax.broadcasted_iota(jnp.int32, (8, RANK), 0)
    live = row[8:] < live_from
    columns = [jnp.broadcast_to(gram[:, k:k + 1], (size, RANK)) for k in range(8)]
    top = [column[:8] for column in columns]
    below = [jnp.where(live, column[8:], 0.0) for column in columns]
    gram8, inverse8 = gram[:8], inverse[:8]
    gram_rest, inverse_rest = gram[8:], inverse[8:]
    pivots = []
    for k in range(8):
        pivot = jnp.broadcast_to(top[k][k:k + 1], (8, RANK))
        reciprocal = 1.0 / pivot
        pivots.append(pivot[:1])
        factor8 = jnp.where(row8 > k, top[k] * reciprocal, 0.0)
        factor = below[k] * reciprocal[:1]
        for j in range(k + 1, 8):
            upper = top[j][k:k + 1]
            top[j] = top[j] - factor8 * upper
            below[j] = below[j] - factor * upper
        gram_row, inverse_row = gram8[k:k + 1], inverse8[k:k + 1]
        gram_rest = gram_rest - factor * gram_row
        inverse_rest = inverse_rest - factor * inverse_row
        gram8 = gram8 - factor8 * gram_row
        inverse8 = inverse8 - factor8 * inverse_row
    done = inverse8 * lax.rsqrt(jnp.concatenate(pivots, 0))
    gram = pltpu.roll(jnp.concatenate([gram_rest, gram8], 0), RANK - 8, 1)
    return gram, jnp.concatenate([inverse_rest, inverse8], 0), done


def split(value):
    high = value.astype(jnp.bfloat16)
    return high, (value - high.astype(jnp.float32)).astype(jnp.bfloat16)


def land(ref, sem):
    pltpu.make_async_copy(ref, ref, sem).wait()


def exchange_kernel(g_hbm, m_hbm, f_hbm, new_ref, n_ref,
                    gm, f, gmt, part, part_y, part_z, span_all, span, span2, o2,
                    gram, gram_in, gram_x, gram_back, lower, work, inverse, x, core_in, a_in, z_in,
                    load_sem, party_send, party_recv, part_send, part_recv, span_send, span_recv,
                    gram_send, gram_recv, core_send, core_recv, a_send, a_recv, z_send, z_recv,
                    gz_send, gz_recv, ga_send, ga_recv, gc_send, gc_recv):
    dp, shard = lax.axis_index("dp"), lax.axis_index("shard")
    zi, yi = dp // YS, dp % YS
    xi, ci = shard // CORES, shard % CORES
    a = xi * (1 - ci) + yi * ci
    b = yi * (1 - ci) + xi * ci

    def plane_peer(j):
        return (j, shard)

    def a_peer(k):
        return (zi * YS + (yi + k * ci) % 4, ((xi + k * (1 - ci)) % 4) * CORES + ci)

    def y_peer(k):
        return (zi * YS + (yi + k) % YS, shard)

    def bz_peer(flip, kz):
        at = flipped(b, flip)
        return (((zi + kz) % ZS) * YS + yi * ci + at * (1 - ci), (xi * (1 - ci) + at * ci) * CORES + ci)

    def xz_peer(kx, kz):
        return (((zi + kz) % ZS) * YS + yi, ((xi + kx) % 4) * CORES + ci)

    sibling = (dp, xi * CORES + 1 - ci)

    def send(src, dst, send_sem, recv_sem, to):
        pltpu.make_async_remote_copy(src_ref=src, dst_ref=dst, send_sem=send_sem, recv_sem=recv_sem,
                                     device_id=to, device_id_type=MESH).start()

    def greet(to):
        pl.semaphore_signal(barrier, inc=1, device_id=to, device_id_type=MESH)


    def quarter(i):
        return (yi + FAR[i]) % 4

    def loads(i):
        q = quarter(i)
        rows = pl.ds(pl.multiple_of(q * 96, 96), 96)
        first = pl.ds(pl.multiple_of(q * 192, 96), 96)
        second = pl.ds(pl.multiple_of(q * 192 + 96, 96), 96)
        return (pltpu.make_async_copy(g_hbm.at[rows], gm.at[first], load_sem.at[2 * i]),
                pltpu.make_async_copy(m_hbm.at[rows], gm.at[second], load_sem.at[2 * i + 1]))

    load_f = pltpu.make_async_copy(f_hbm, f, load_sem.at[8])
    load_f.start()
    for i in range(2):
        for copy in loads(i):
            copy.start()

    barrier = pltpu.get_barrier_semaphore()
    for k in (4, 3, 5, 2, 6, 1, 7):
        greet(xz_peer(0, k))
    for k in (2, 1, 3):
        greet(y_peer(k))
        greet(xz_peer(k, 0))
    greet(sibling)

    load_f.wait()
    for i in range(4):
        q = quarter(i)
        for copy in loads(i):
            copy.wait()
        if i < 2:
            for copy in loads(i + 2):
                copy.start()
        both = jnp.dot(gm[pl.ds(pl.multiple_of(q * 192, 192), 192), :], f[...], preferred_element_type=jnp.float32)
        value = both[:96] + both[96:]
        for j in range(ZS):
            part[q * ZS + j] = value[PIECE * j:PIECE * (j + 1)]
        if i == 0:
            pl.semaphore_wait(barrier, 14)
        if FAR[i]:
            send(part.at[pl.ds(q * ZS, ZS)], part_y.at[i], party_send, party_recv.at[i], y_peer(FAR[i]))

    def turn(i, _):
        lanes = pl.ds(pl.multiple_of(i * 128, 128), 128)
        gmt[lanes, :] = gm[:, lanes].T
        return 0
    lax.fori_loop(0, BLOCKS // 2, turn, 0)
    for i in range(3):
        land(part_y.at[i], party_recv.at[i])
    for j in range(ZS):
        to = (zi + FAR_Z[j]) % ZS
        slot = yi * ZS + to
        part[slot] = (part[slot] + part_y[0, to]) + (part_y[1, to] + part_y[2, to])
        if FAR_Z[j]:
            send(part.at[slot], part_z.at[FAR_Z[j] - 1], part_send, part_recv, xz_peer(0, FAR_Z[j]))
    lax.fori_loop(BLOCKS // 2, BLOCKS, turn, 0)
    gmt[D:, :] = jnp.zeros((PADDED - D, 2 * ROWS), jnp.bfloat16)

    me = yi * ZS + zi
    land(part_z, part_recv)
    total = part[me]
    for k in range(ZS - 1):
        total = total + part_z[k]
    span_all[me] = total * (1.0 / DP)

    def spread(k, _):
        send(span_all.at[me], span_all.at[me], span_send, span_recv, plane_peer((dp + k) % DP))
        return 0
    lax.fori_loop(10, 23, spread, 0)
    lax.fori_loop(1, 10, spread, 0)
    lax.fori_loop(23, DP, spread, 0)
    land(span_all.at[pl.ds(0, DP - 1)], span_recv)

    for j in range(DP // 2):
        span[24 * j:24 * (j + 1), :] = jnp.concatenate([span_all[2 * j], span_all[2 * j + 1]], 0)
    for q in range(4):
        high, low = split(span[96 * q:96 * (q + 1), :])
        for start in (192 * q, 192 * q + 96):
            span2[start:start + 96, :RANK] = high
            span2[start:start + 96, RANK:] = low

    mine = pl.ds(pl.multiple_of(ci * 64, 64), 64)
    other = pl.ds(pl.multiple_of((1 - ci) * 64, 64), 64)

    def product(start):
        both = jnp.dot(gmt[pl.ds(start, BIG), :], span2[...], preferred_element_type=jnp.float32)
        return both[:, :RANK] + both[:, RANK:]

    def for_sibling(i):
        start = pl.multiple_of((1 - ci) * HALF + ((b + FAR[i]) % 4) * BIG, BIG)
        x[pl.ds(start, BIG), :] = product(start)
        send(x.at[pl.ds(start, BIG)], core_in.at[i], core_send, core_recv.at[i], sibling)

    def pair_of(core, first, half, pair):
        return pl.multiple_of(core * HALF + first * BIG + half * HALF_BIG + pair * PAIR, PAIR)

    def group_of(core, first, half, second):
        return pl.multiple_of(core * HALF + first * BIG + half * HALF_BIG + second * GROUP, GROUP)

    def flipped(place, flip):
        return (place // 2 + flip // 2) % 2 * 2 + (place + flip) % 2

    def to_axis(i, half):
        for flip in (3, 2, 1, 0):
            rows = pl.ds(group_of(ci, (a + FAR[i]) % 4, half, flipped(b, flip)), GROUP)
            send(x.at[rows], a_in.at[i, half, flip], a_send, a_recv.at[i, half, flip], a_peer(FAR[i]))

    def for_axis(i):
        start = pl.multiple_of(ci * HALF + ((a + FAR[i]) % 4) * BIG, BIG)
        value = product(start)
        land(core_in.at[i], core_recv.at[i])
        x[pl.ds(start, BIG), :] = value + core_in[i]
        if FAR[i]:
            to_axis(i, 0)

    gram[...] = lax.dot_general(span[...], span[...], (((0,), (0,)), ((), ())),
                                precision=lax.Precision.HIGHEST, preferred_element_type=jnp.float32)
    send(gram.at[other], gram_in, gram_send.at[0], gram_recv.at[0], sibling)
    for_sibling(0)
    for_sibling(1)
    land(gram_in, gram_recv.at[0])
    gram[mine, :] = gram[mine, :] + gram_in[...]
    for r in (1, 2, 3):
        send(gram.at[mine], gram_x.at[r - 1], gram_send.at[1], gram_recv.at[1], xz_peer(r, 0))
    for_axis(0)
    for_sibling(2)
    for_axis(1)
    for_sibling(3)
    for_axis(2)
    for i in range(3):
        to_axis(i, 1)
    for_axis(3)
    row = lax.broadcasted_iota(jnp.int32, (RANK, RANK), 0)
    lane = lax.broadcasted_iota(jnp.int32, (RANK, RANK), 1)
    work[...] = (row == lane).astype(jnp.float32)

    def eliminate(first, last):
        size = RANK - 32 * (first // 4)

        def one(step, _):
            rows = pl.ds(pl.multiple_of(step * 8, 8), 8)
            lower[:size, :], work[:size, :], inverse[rows, :] = eight_columns(
                RANK - 8 * step, lower[:size, :], work[:size, :])
            return 0
        lax.fori_loop(first, last, one, 0)

    def to_owners(half, flip):
        block = group_of(ci, a, half, flipped(b, flip))
        rows = pl.ds(block, GROUP)
        for i in range(3):
            land(a_in.at[i, half, flip], a_recv.at[i, half, flip])
        x[rows, :] = x[rows, :] + a_in[0, half, flip] + a_in[1, half, flip] + a_in[2, half, flip]
        for kz in FAR_Z:
            if flip or kz:
                piece = pl.ds(pl.multiple_of(block + (zi + kz) % ZS * SMALL, SMALL), SMALL)
                slot = ZS * (3 - flip) + kz - (1 if flip == 0 else 0)
                send(x.at[piece], z_in.at[half, slot], z_send, z_recv.at[half], bz_peer(flip, kz))

    to_owners(0, 3)
    to_owners(0, 2)
    land(gram_x, gram_recv.at[1])
    land(gram_x, gram_send.at[1])
    gram[mine, :] = gram[mine, :] + gram_x[0] + gram_x[1] + gram_x[2]
    send(gram.at[mine], gram_back, gram_send.at[2], gram_recv.at[2], sibling)
    lower[mine, :] = gram[mine, :]
    to_owners(0, 1)
    to_owners(0, 0)
    land(gram_back, gram_recv.at[2])
    lower[other, :] = gram_back[...]
    eliminate(0, 1)
    to_owners(1, 3)
    eliminate(1, 2)
    to_owners(1, 2)
    eliminate(2, 3)
    to_owners(1, 1)
    eliminate(3, 4)
    to_owners(1, 0)
    eliminate(4, 8)
    eliminate(8, 12)
    eliminate(12, 16)

    def spread_rows(half):
        rows = pl.ds(pl.multiple_of(group_of(ci, a, half, b) + zi * SMALL, SMALL), SMALL)
        land(z_in.at[half], z_recv.at[half])
        total = x[rows, :]
        for k in range(4 * ZS - 1):
            total = total + z_in[half, k]
        n_ref[rows, :] = lax.dot_general(total * (1.0 / DP), inverse[...], (((1,), (1,)), ((), ())),
                                         precision=lax.Precision.HIGHEST, preferred_element_type=jnp.float32)
        for flip in range(4):
            for kz in FAR_Z:
                if flip or kz:
                    send(n_ref.at[rows], n_ref.at[rows], gz_send, gz_recv.at[half, flip], bz_peer(flip, kz))

    spread_rows(0)
    span_in_basis = lax.dot_general(span[...], inverse[...], (((1,), (1,)), ((), ())),
                                    precision=lax.Precision.HIGHEST, preferred_element_type=jnp.float32)
    high, low = split(span_in_basis)
    o2[:, :RANK] = high
    o2[:, RANK:] = low
    spread_rows(1)

    def residual(start, width):
        @pl.when(start < D)
        def _():
            cols = pl.ds(start, width)
            high, low = split(n_ref[cols, :])
            update = (lax.dot_general(o2[...], jnp.concatenate([high, high], 1), (((1,), (1,)), ((), ())),
                                      preferred_element_type=jnp.float32)
                      + lax.dot_general(o2[:, :RANK], low, (((1,), (1,)), ((), ())),
                                        preferred_element_type=jnp.float32))
            for q in range(4):
                corrected = (gm[192 * q:192 * q + 96, cols].astype(jnp.float32)
                             + gm[192 * q + 96:192 * q + 192, cols].astype(jnp.float32))
                new_ref[96 * q:96 * (q + 1), cols] = (corrected - update[96 * q:96 * (q + 1)]).astype(jnp.bfloat16)

    def from_owners(half, flip):
        rows = pl.ds(group_of(ci, a, half, flipped(b, flip)), GROUP)
        land(n_ref.at[pl.ds(0, GROUP - (SMALL if flip == 0 else 0))], gz_recv.at[half, flip])
        for r in range(3):
            send(n_ref.at[rows], n_ref.at[rows], ga_send, ga_recv.at[r, half, flip], a_peer(FAR[r]))
        send(n_ref.at[rows], n_ref.at[rows], gc_send, gc_recv.at[3, half, flip], sibling)

    def from_axis(half, flip):
        for i in (1, 2, 0):
            rows = pl.ds(group_of(ci, (a - FAR[i] + 4) % 4, half, flipped(b, flip)), GROUP)
            land(n_ref.at[rows], ga_recv.at[i, half, flip])
            send(n_ref.at[rows], n_ref.at[rows], gc_send, gc_recv.at[i, half, flip], sibling)

    def from_sibling(i, half, flips):
        for flip in flips:
            land(n_ref.at[pl.ds(0, GROUP)], gc_recv.at[i, half, flip])

    DISTANCES = FAR[:3] + (0,)

    def own_columns(i, half, p=None):
        if p is None:
            residual(pl.multiple_of(pair_of(ci, (a - DISTANCES[i] + 4) % 4, half, 0), HALF_BIG), HALF_BIG)
        else:
            residual(pair_of(ci, (a - DISTANCES[i] + 4) % 4, half, (b // 2 + p) % 2), PAIR)

    def sibling_columns(i, half, p=None):
        if p is None:
            residual(pl.multiple_of(pair_of(1 - ci, (b - DISTANCES[i] + 4) % 4, half, 0), HALF_BIG), HALF_BIG)
        else:
            residual(pair_of(1 - ci, (b - DISTANCES[i] + 4) % 4, half, (a // 2 + p) % 2), PAIR)

    from_owners(0, 0)
    from_owners(0, 1)
    own_columns(3, 0, 0)
    from_owners(1, 0)
    from_owners(0, 2)
    from_owners(0, 3)
    own_columns(3, 0, 1)
    from_axis(0, 0)
    from_owners(1, 1)
    own_columns(3, 1, 0)
    from_axis(0, 1)
    from_owners(1, 2)
    from_axis(1, 0)
    from_owners(1, 3)
    own_columns(3, 1, 1)
    from_axis(0, 2)
    from_axis(0, 3)
    for i in range(3):
        own_columns(i, 0)
    from_axis(1, 1)
    for i in (3, 1, 2, 0):
        from_sibling(i, 0, range(4))
        sibling_columns(i, 0)
    from_axis(1, 2)
    for i in range(3):
        own_columns(i, 1, 0)
    from_axis(1, 3)
    for i in (3, 1, 2, 0):
        from_sibling(i, 1, (0, 1))
        sibling_columns(i, 1, 0)
    for i in range(3):
        own_columns(i, 1, 1)
    for i in (3, 1, 2, 0):
        from_sibling(i, 1, (2, 3))
        sibling_columns(i, 1, 1)

    land(part_y, party_send)
    land(part_z, part_send)
    land(span_all.at[pl.ds(0, DP - 1)], span_send)
    land(gram_in, gram_send.at[0])
    land(gram_in, gram_send.at[2])
    land(x.at[pl.ds(0, HALF)], core_send)
    land(a_in, a_send)
    land(z_in, z_send)
    land(z_in, gz_send)
    land(a_in, ga_send)
    land(x.at[pl.ds(0, HALF)], gc_send)


def exchange(g, m, f):
    dma = pltpu.SemaphoreType.DMA
    f32, bf16 = jnp.float32, jnp.bfloat16
    return pl.pallas_call(
        exchange_kernel,
        out_shape=(jax.ShapeDtypeStruct((ROWS, D), bf16), jax.ShapeDtypeStruct((PADDED, RANK), f32)),
        in_specs=[pl.BlockSpec(memory_space=pltpu.HBM)] * 3,
        out_specs=(pl.BlockSpec(memory_space=pltpu.VMEM), pl.BlockSpec(memory_space=pltpu.VMEM)),
        scratch_shapes=[
            pltpu.VMEM((2 * ROWS, D), bf16), pltpu.VMEM((D, RANK), bf16), pltpu.VMEM((PADDED, 2 * ROWS), bf16),
            pltpu.VMEM((DP, PIECE, RANK), f32), pltpu.VMEM((3, ZS, PIECE, RANK), f32),
            pltpu.VMEM((ZS - 1, PIECE, RANK), f32),
            pltpu.VMEM((DP, PIECE, RANK), f32), pltpu.VMEM((ROWS, RANK), f32),
            pltpu.VMEM((2 * ROWS, 2 * RANK), bf16), pltpu.VMEM((ROWS, 2 * RANK), bf16),
            pltpu.VMEM((RANK, RANK), f32), pltpu.VMEM((64, RANK), f32), pltpu.VMEM((3, 64, RANK), f32),
            pltpu.VMEM((64, RANK), f32), pltpu.VMEM((RANK, RANK), f32), pltpu.VMEM((RANK, RANK), f32),
            pltpu.VMEM((RANK, RANK), f32),
            pltpu.VMEM((PADDED, RANK), f32), pltpu.VMEM((4, BIG, RANK), f32),
            pltpu.VMEM((3, 2, 4, GROUP, RANK), f32), pltpu.VMEM((2, 4 * ZS - 1, SMALL, RANK), f32),
            dma((9,)), dma, dma((3,)), dma, dma, dma, dma, dma((3,)), dma((3,)), dma, dma((4,)), dma, dma((3, 2, 4)), dma, dma((2,)),
            dma, dma((2, 4)), dma, dma((3, 2, 4)), dma, dma((4, 2, 4)),
        ],
        compiler_params=pltpu.CompilerParams(collective_id=0, has_side_effects=True, vmem_limit_bytes=VMEM_BYTES),
        name="exchange",
    )(g, m, f)


def store_kernel(new_ref, n_ref, memory_ref, factor_ref, sems):
    copies = [pltpu.make_async_copy(new_ref.at[pl.ds(96 * i, 96)], memory_ref.at[pl.ds(96 * i, 96)], sems.at[i])
              for i in range(4)]
    quarter = D // 4
    copies += [pltpu.make_async_copy(n_ref.at[pl.ds(quarter * i, quarter)], factor_ref.at[pl.ds(quarter * i, quarter)],
                                     sems.at[4 + i]) for i in range(4)]
    for copy in copies:
        copy.start()
    for copy in copies:
        copy.wait()


def store(new, n):
    return pl.pallas_call(
        store_kernel,
        out_shape=(jax.ShapeDtypeStruct((ROWS, D), jnp.bfloat16), jax.ShapeDtypeStruct((D, RANK), jnp.float32)),
        in_specs=[pl.BlockSpec(memory_space=pltpu.VMEM)] * 2,
        out_specs=(pl.BlockSpec(memory_space=pltpu.HBM), pl.BlockSpec(memory_space=pltpu.HBM)),
        scratch_shapes=[pltpu.SemaphoreType.DMA((8,))],
        compiler_params=pltpu.CompilerParams(vmem_limit_bytes=STORE_VMEM),
        name="store",
    )(new, n)


def per_device(gradient, memory, old_factor):
    new_memory, new_factor = store(*exchange(gradient[0], memory[0], pltpu.with_memory_space_constraint(old_factor, pltpu.HBM)))
    return (new_memory[None], new_factor)


def solution(mesh):
    in_specs = (P("dp", "shard", None), P("dp", "shard", None), P())
    out_specs = (P("dp", "shard", None), P())
    return jax.shard_map(
        per_device, mesh=mesh, in_specs=in_specs, out_specs=out_specs, check_vma=False
    )
```

```python
import functools

import jax
import jax.numpy as jnp
from jax import lax
from jax.experimental import pallas as pl
from jax.experimental.pallas import tpu as pltpu
from jax.sharding import PartitionSpec as P

MESH = pl.DeviceIdType.MESH
D = 3968
RANK = 128
ROWS = 384
ZS, YS, XS, CORES = 8, 4, 4, 2
DP = ZS * YS
PIECE = ROWS // DP
PADDED = 4096
HALF = PADDED // CORES
BIG = HALF // 4
HALF_BIG = BIG // 2
PAIR = HALF_BIG // 2
GROUP = PAIR // 2
SMALL = GROUP // ZS
BLOCKS = D // 128
FAR = (2, 1, 3, 0)
FAR_Z = (4, 3, 5, 2, 6, 1, 7, 0)
VMEM_BYTES = 48 * 1024 * 1024
STORE_VMEM = 16 * 1024 * 1024


def eight_columns(live_from, gram, inverse):
    size = gram.shape[0]
    row = lax.broadcasted_iota(jnp.int32, (size, 1), 0)
    row8 = lax.broadcasted_iota(jnp.int32, (8, RANK), 0)
    live = row[8:] < live_from
    columns = [jnp.broadcast_to(gram[:, k:k + 1], (size, RANK)) for k in range(8)]
    top = [column[:8] for column in columns]
    below = [jnp.where(live, column[8:], 0.0) for column in columns]
    gram8, inverse8 = gram[:8], inverse[:8]
    gram_rest, inverse_rest = gram[8:], inverse[8:]
    pivots = []
    for k in range(8):
        pivot = jnp.broadcast_to(top[k][k:k + 1], (8, RANK))
        reciprocal = 1.0 / pivot
        pivots.append(pivot[:1])
        factor8 = jnp.where(row8 > k, top[k] * reciprocal, 0.0)
        factor = below[k] * reciprocal[:1]
        for j in range(k + 1, 8):
            upper = top[j][k:k + 1]
            top[j] = top[j] - factor8 * upper
            below[j] = below[j] - factor * upper
        gram_row, inverse_row = gram8[k:k + 1], inverse8[k:k + 1]
        gram_rest = gram_rest - factor * gram_row
        inverse_rest = inverse_rest - factor * inverse_row
        gram8 = gram8 - factor8 * gram_row
        inverse8 = inverse8 - factor8 * inverse_row
    done = inverse8 * lax.rsqrt(jnp.concatenate(pivots, 0))
    gram = pltpu.roll(jnp.concatenate([gram_rest, gram8], 0), RANK - 8, 1)
    return gram, jnp.concatenate([inverse_rest, inverse8], 0), done


def split(value):
    high = value.astype(jnp.bfloat16)
    return high, (value - high.astype(jnp.float32)).astype(jnp.bfloat16)


def land(ref, sem):
    pltpu.make_async_copy(ref, ref, sem).wait()


def exchange_kernel(g_hbm, m_hbm, f_hbm, new_ref, n_ref,
                    gm, f, gmt, part, part_y, part_z, span_all, span, span2, o2,
                    gram, gram_in, gram_x, gram_back, lower, work, inverse, x, core_in, a_in, z_in,
                    load_sem, party_send, party_recv, part_send, part_recv, span_send, span_recv,
                    gram_send, gram_recv, core_send, core_recv, a_send, a_recv, z_send, z_recv,
                    gz_send, gz_recv, ga_send, ga_recv, gc_send, gc_recv):
    dp, shard = lax.axis_index("dp"), lax.axis_index("shard")
    zi, yi = dp // YS, dp % YS
    xi, ci = shard // CORES, shard % CORES
    a = xi * (1 - ci) + yi * ci
    b = yi * (1 - ci) + xi * ci

    def plane_peer(j):
        return (j, shard)

    def a_peer(k):
        return (zi * YS + (yi + k * ci) % 4, ((xi + k * (1 - ci)) % 4) * CORES + ci)

    def y_peer(k):
        return (zi * YS + (yi + k) % YS, shard)

    def bz_peer(flip, kz):
        at = flipped(b, flip)
        return (((zi + kz) % ZS) * YS + yi * ci + at * (1 - ci), (xi * (1 - ci) + at * ci) * CORES + ci)

    def xz_peer(kx, kz):
        return (((zi + kz) % ZS) * YS + yi, ((xi + kx) % 4) * CORES + ci)

    sibling = (dp, xi * CORES + 1 - ci)

    def send(src, dst, send_sem, recv_sem, to):
        pltpu.make_async_remote_copy(src_ref=src, dst_ref=dst, send_sem=send_sem, recv_sem=recv_sem,
                                     device_id=to, device_id_type=MESH).start()

    def greet(to):
        pl.semaphore_signal(barrier, inc=1, device_id=to, device_id_type=MESH)


    def quarter(i):
        return (yi + FAR[i]) % 4

    def loads(i):
        q = quarter(i)
        rows = pl.ds(pl.multiple_of(q * 96, 96), 96)
        first = pl.ds(pl.multiple_of(q * 192, 96), 96)
        second = pl.ds(pl.multiple_of(q * 192 + 96, 96), 96)
        return (pltpu.make_async_copy(g_hbm.at[rows], gm.at[first], load_sem.at[2 * i]),
                pltpu.make_async_copy(m_hbm.at[rows], gm.at[second], load_sem.at[2 * i + 1]))

    load_f = pltpu.make_async_copy(f_hbm, f, load_sem.at[8])
    load_f.start()
    for i in range(2):
        for copy in loads(i):
            copy.start()

    barrier = pltpu.get_barrier_semaphore()
    for k in (4, 3, 5, 2, 6, 1, 7):
        greet(xz_peer(0, k))
    for k in (2, 1, 3):
        greet(y_peer(k))
        greet(xz_peer(k, 0))
    greet(sibling)

    load_f.wait()
    for i in range(4):
        q = quarter(i)
        for copy in loads(i):
            copy.wait()
        if i < 2:
            for copy in loads(i + 2):
                copy.start()
        both = jnp.dot(gm[pl.ds(pl.multiple_of(q * 192, 192), 192), :], f[...], preferred_element_type=jnp.float32)
        value = both[:96] + both[96:]
        for j in range(ZS):
            part[q * ZS + j] = value[PIECE * j:PIECE * (j + 1)]
        if i == 0:
            pl.semaphore_wait(barrier, 14)
        if FAR[i]:
            send(part.at[pl.ds(q * ZS, ZS)], part_y.at[i], party_send, party_recv.at[i], y_peer(FAR[i]))

    def turn(i, _):
        lanes = pl.ds(pl.multiple_of(i * 128, 128), 128)
        gmt[lanes, :] = gm[:, lanes].T
        return 0
    lax.fori_loop(0, BLOCKS // 2, turn, 0)
    for i in range(3):
        land(part_y.at[i], party_recv.at[i])
    for j in range(ZS):
        to = (zi + FAR_Z[j]) % ZS
        slot = yi * ZS + to
        part[slot] = (part[slot] + part_y[0, to]) + (part_y[1, to] + part_y[2, to])
        if FAR_Z[j]:
            send(part.at[slot], part_z.at[FAR_Z[j] - 1], part_send, part_recv, xz_peer(0, FAR_Z[j]))
    lax.fori_loop(BLOCKS // 2, BLOCKS, turn, 0)
    gmt[D:, :] = jnp.zeros((PADDED - D, 2 * ROWS), jnp.bfloat16)

    me = yi * ZS + zi
    land(part_z, part_recv)
    total = part[me]
    for k in range(ZS - 1):
        total = total + part_z[k]
    span_all[me] = total * (1.0 / DP)

    def spread(k, _):
        send(span_all.at[me], span_all.at[me], span_send, span_recv, plane_peer((dp + k) % DP))
        return 0
    lax.fori_loop(10, 23, spread, 0)
    lax.fori_loop(1, 10, spread, 0)
    lax.fori_loop(23, DP, spread, 0)
    land(span_all.at[pl.ds(0, DP - 1)], span_recv)

    for j in range(DP // 2):
        span[24 * j:24 * (j + 1), :] = jnp.concatenate([span_all[2 * j], span_all[2 * j + 1]], 0)
    for q in range(4):
        high, low = split(span[96 * q:96 * (q + 1), :])
        for start in (192 * q, 192 * q + 96):
            span2[start:start + 96, :RANK] = high
            span2[start:start + 96, RANK:] = low

    mine = pl.ds(pl.multiple_of(ci * 64, 64), 64)
    other = pl.ds(pl.multiple_of((1 - ci) * 64, 64), 64)

    def product(start):
        both = jnp.dot(gmt[pl.ds(start, BIG), :], span2[...], preferred_element_type=jnp.float32)
        return both[:, :RANK] + both[:, RANK:]

    def for_sibling(i):
        start = pl.multiple_of((1 - ci) * HALF + ((b + FAR[i]) % 4) * BIG, BIG)
        x[pl.ds(start, BIG), :] = product(start)
        send(x.at[pl.ds(start, BIG)], core_in.at[i], core_send, core_recv.at[i], sibling)

    def pair_of(core, first, half, pair):
        return pl.multiple_of(core * HALF + first * BIG + half * HALF_BIG + pair * PAIR, PAIR)

    def group_of(core, first, half, second):
        return pl.multiple_of(core * HALF + first * BIG + half * HALF_BIG + second * GROUP, GROUP)

    def flipped(place, flip):
        return (place // 2 + flip // 2) % 2 * 2 + (place + flip) % 2

    def to_axis(i, half):
        for flip in (3, 2, 1, 0):
            rows = pl.ds(group_of(ci, (a + FAR[i]) % 4, half, flipped(b, flip)), GROUP)
            send(x.at[rows], a_in.at[i, half, flip], a_send, a_recv.at[i, half, flip], a_peer(FAR[i]))

    def for_axis(i):
        start = pl.multiple_of(ci * HALF + ((a + FAR[i]) % 4) * BIG, BIG)
        value = product(start)
        land(core_in.at[i], core_recv.at[i])
        x[pl.ds(start, BIG), :] = value + core_in[i]
        if FAR[i]:
            to_axis(i, 0)

    gram[...] = lax.dot_general(span[...], span[...], (((0,), (0,)), ((), ())),
                                precision=lax.Precision.HIGHEST, preferred_element_type=jnp.float32)
    send(gram.at[other], gram_in, gram_send.at[0], gram_recv.at[0], sibling)
    for_sibling(0)
    for_sibling(1)
    land(gram_in, gram_recv.at[0])
    gram[mine, :] = gram[mine, :] + gram_in[...]
    for r in (1, 2, 3):
        send(gram.at[mine], gram_x.at[r - 1], gram_send.at[1], gram_recv.at[1], xz_peer(r, 0))
    for_axis(0)
    for_sibling(2)
    for_axis(1)
    for_sibling(3)
    for_axis(2)
    for i in range(3):
        to_axis(i, 1)
    for_axis(3)
    row = lax.broadcasted_iota(jnp.int32, (RANK, RANK), 0)
    lane = lax.broadcasted_iota(jnp.int32, (RANK, RANK), 1)
    work[...] = (row == lane).astype(jnp.float32)

    def eliminate(first, last):
        size = RANK - 32 * (first // 4)

        def one(step, _):
            rows = pl.ds(pl.multiple_of(step * 8, 8), 8)
            lower[:size, :], work[:size, :], inverse[rows, :] = eight_columns(
                RANK - 8 * step, lower[:size, :], work[:size, :])
            return 0
        lax.fori_loop(first, last, one, 0)

    def to_owners(half, flip):
        block = group_of(ci, a, half, flipped(b, flip))
        rows = pl.ds(block, GROUP)
        for i in range(3):
            land(a_in.at[i, half, flip], a_recv.at[i, half, flip])
        x[rows, :] = x[rows, :] + a_in[0, half, flip] + a_in[1, half, flip] + a_in[2, half, flip]
        for kz in FAR_Z:
            if flip or kz:
                piece = pl.ds(pl.multiple_of(block + (zi + kz) % ZS * SMALL, SMALL), SMALL)
                slot = ZS * (3 - flip) + kz - (1 if flip == 0 else 0)
                send(x.at[piece], z_in.at[half, slot], z_send, z_recv.at[half], bz_peer(flip, kz))

    to_owners(0, 3)
    to_owners(0, 2)
    land(gram_x, gram_recv.at[1])
    land(gram_x, gram_send.at[1])
    gram[mine, :] = gram[mine, :] + gram_x[0] + gram_x[1] + gram_x[2]
    send(gram.at[mine], gram_back, gram_send.at[2], gram_recv.at[2], sibling)
    lower[mine, :] = gram[mine, :]
    to_owners(0, 1)
    to_owners(0, 0)
    land(gram_back, gram_recv.at[2])
    lower[other, :] = gram_back[...]
    eliminate(0, 1)
    to_owners(1, 3)
    eliminate(1, 2)
    to_owners(1, 2)
    eliminate(2, 3)
    to_owners(1, 1)
    eliminate(3, 4)
    to_owners(1, 0)
    eliminate(4, 8)
    eliminate(8, 12)
    eliminate(12, 16)

    def spread_rows(half):
        rows = pl.ds(pl.multiple_of(group_of(ci, a, half, b) + zi * SMALL, SMALL), SMALL)
        land(z_in.at[half], z_recv.at[half])
        total = x[rows, :]
        for k in range(4 * ZS - 1):
            total = total + z_in[half, k]
        n_ref[rows, :] = lax.dot_general(total * (1.0 / DP), inverse[...], (((1,), (1,)), ((), ())),
                                         precision=lax.Precision.HIGHEST, preferred_element_type=jnp.float32)
        for flip in range(4):
            for kz in FAR_Z:
                if flip or kz:
                    send(n_ref.at[rows], n_ref.at[rows], gz_send, gz_recv.at[half, flip], bz_peer(flip, kz))

    spread_rows(0)
    span_in_basis = lax.dot_general(span[...], inverse[...], (((1,), (1,)), ((), ())),
                                    precision=lax.Precision.HIGHEST, preferred_element_type=jnp.float32)
    high, low = split(span_in_basis)
    o2[:, :RANK] = high
    o2[:, RANK:] = low
    spread_rows(1)

    def residual(start, width):
        @pl.when(start < D)
        def _():
            cols = pl.ds(start, width)
            high, low = split(n_ref[cols, :])
            update = (lax.dot_general(o2[...], jnp.concatenate([high, high], 1), (((1,), (1,)), ((), ())),
                                      preferred_element_type=jnp.float32)
                      + lax.dot_general(o2[:, :RANK], low, (((1,), (1,)), ((), ())),
                                        preferred_element_type=jnp.float32))
            for q in range(4):
                corrected = (gm[192 * q:192 * q + 96, cols].astype(jnp.float32)
                             + gm[192 * q + 96:192 * q + 192, cols].astype(jnp.float32))
                new_ref[96 * q:96 * (q + 1), cols] = (corrected - update[96 * q:96 * (q + 1)]).astype(jnp.bfloat16)

    def from_owners(half, flip):
        rows = pl.ds(group_of(ci, a, half, flipped(b, flip)), GROUP)
        land(n_ref.at[pl.ds(0, GROUP - (SMALL if flip == 0 else 0))], gz_recv.at[half, flip])
        for r in range(3):
            send(n_ref.at[rows], n_ref.at[rows], ga_send, ga_recv.at[r, half, flip], a_peer(FAR[r]))
        send(n_ref.at[rows], n_ref.at[rows], gc_send, gc_recv.at[3, half, flip], sibling)

    def from_axis(half, flip):
        for i in (1, 2, 0):
            rows = pl.ds(group_of(ci, (a - FAR[i] + 4) % 4, half, flipped(b, flip)), GROUP)
            land(n_ref.at[rows], ga_recv.at[i, half, flip])
            send(n_ref.at[rows], n_ref.at[rows], gc_send, gc_recv.at[i, half, flip], sibling)

    def from_sibling(i, half, flips):
        for flip in flips:
            land(n_ref.at[pl.ds(0, GROUP)], gc_recv.at[i, half, flip])

    DISTANCES = FAR[:3] + (0,)

    def whole(core, first, half):
        start = pl.multiple_of(pair_of(core, first, half, 0), HALF_BIG)
        if half == 0:
            residual(start, HALF_BIG)
        else:
            @pl.when(start + HALF_BIG <= D)
            def _():
                residual(start, HALF_BIG)

            @pl.when(start + HALF_BIG > D)
            def _():
                residual(pl.multiple_of(start, PAIR), PAIR)

    def own_columns(i, half):
        whole(ci, (a - DISTANCES[i] + 4) % 4, half)

    def sibling_columns(i, half):
        whole(1 - ci, (b - DISTANCES[i] + 4) % 4, half)

    from_owners(0, 0)
    from_owners(0, 1)
    from_owners(1, 0)
    from_owners(0, 2)
    from_owners(0, 3)
    from_axis(0, 0)
    own_columns(3, 0)
    from_owners(1, 1)
    from_axis(0, 1)
    from_owners(1, 2)
    from_axis(1, 0)
    from_owners(1, 3)
    own_columns(3, 1)
    from_axis(0, 2)
    from_axis(0, 3)
    for i in range(3):
        own_columns(i, 0)
    from_axis(1, 1)
    for i in (3, 1, 2, 0):
        from_sibling(i, 0, range(4))
        sibling_columns(i, 0)
    from_axis(1, 2)
    from_axis(1, 3)
    from_sibling(3, 1, range(4))
    sibling_columns(3, 1)
    for i in range(3):
        own_columns(i, 1)
    for i in (1, 2, 0):
        from_sibling(i, 1, range(4))
        sibling_columns(i, 1)

    land(part_y, party_send)
    land(part_z, part_send)
    land(span_all.at[pl.ds(0, DP - 1)], span_send)
    land(gram_in, gram_send.at[0])
    land(gram_in, gram_send.at[2])
    land(x.at[pl.ds(0, HALF)], core_send)
    land(a_in, a_send)
    land(z_in, z_send)
    land(z_in, gz_send)
    land(a_in, ga_send)
    land(x.at[pl.ds(0, HALF)], gc_send)


def exchange(g, m, f):
    dma = pltpu.SemaphoreType.DMA
    f32, bf16 = jnp.float32, jnp.bfloat16
    return pl.pallas_call(
        exchange_kernel,
        out_shape=(jax.ShapeDtypeStruct((ROWS, D), bf16), jax.ShapeDtypeStruct((PADDED, RANK), f32)),
        in_specs=[pl.BlockSpec(memory_space=pltpu.HBM)] * 3,
        out_specs=(pl.BlockSpec(memory_space=pltpu.VMEM), pl.BlockSpec(memory_space=pltpu.VMEM)),
        scratch_shapes=[
            pltpu.VMEM((2 * ROWS, D), bf16), pltpu.VMEM((D, RANK), bf16), pltpu.VMEM((PADDED, 2 * ROWS), bf16),
            pltpu.VMEM((DP, PIECE, RANK), f32), pltpu.VMEM((3, ZS, PIECE, RANK), f32),
            pltpu.VMEM((ZS - 1, PIECE, RANK), f32),
            pltpu.VMEM((DP, PIECE, RANK), f32), pltpu.VMEM((ROWS, RANK), f32),
            pltpu.VMEM((2 * ROWS, 2 * RANK), bf16), pltpu.VMEM((ROWS, 2 * RANK), bf16),
            pltpu.VMEM((RANK, RANK), f32), pltpu.VMEM((64, RANK), f32), pltpu.VMEM((3, 64, RANK), f32),
            pltpu.VMEM((64, RANK), f32), pltpu.VMEM((RANK, RANK), f32), pltpu.VMEM((RANK, RANK), f32),
            pltpu.VMEM((RANK, RANK), f32),
            pltpu.VMEM((PADDED, RANK), f32), pltpu.VMEM((4, BIG, RANK), f32),
            pltpu.VMEM((3, 2, 4, GROUP, RANK), f32), pltpu.VMEM((2, 4 * ZS - 1, SMALL, RANK), f32),
            dma((9,)), dma, dma((3,)), dma, dma, dma, dma, dma((3,)), dma((3,)), dma, dma((4,)), dma, dma((3, 2, 4)), dma, dma((2,)),
            dma, dma((2, 4)), dma, dma((3, 2, 4)), dma, dma((4, 2, 4)),
        ],
        compiler_params=pltpu.CompilerParams(collective_id=0, has_side_effects=True, vmem_limit_bytes=VMEM_BYTES),
        name="exchange",
    )(g, m, f)


def store_kernel(new_ref, n_ref, memory_ref, factor_ref, sems):
    copies = [pltpu.make_async_copy(new_ref.at[pl.ds(96 * i, 96)], memory_ref.at[pl.ds(96 * i, 96)], sems.at[i])
              for i in range(4)]
    quarter = D // 4
    copies += [pltpu.make_async_copy(n_ref.at[pl.ds(quarter * i, quarter)], factor_ref.at[pl.ds(quarter * i, quarter)],
                                     sems.at[4 + i]) for i in range(4)]
    for copy in copies:
        copy.start()
    for copy in copies:
        copy.wait()


def store(new, n):
    return pl.pallas_call(
        store_kernel,
        out_shape=(jax.ShapeDtypeStruct((ROWS, D), jnp.bfloat16), jax.ShapeDtypeStruct((D, RANK), jnp.float32)),
        in_specs=[pl.BlockSpec(memory_space=pltpu.VMEM)] * 2,
        out_specs=(pl.BlockSpec(memory_space=pltpu.HBM), pl.BlockSpec(memory_space=pltpu.HBM)),
        scratch_shapes=[pltpu.SemaphoreType.DMA((8,))],
        compiler_params=pltpu.CompilerParams(vmem_limit_bytes=STORE_VMEM),
        name="store",
    )(new, n)


def per_device(gradient, memory, old_factor):
    new_memory, new_factor = store(*exchange(gradient[0], memory[0], pltpu.with_memory_space_constraint(old_factor, pltpu.HBM)))
    return (new_memory[None], new_factor)


def solution(mesh):
    in_specs = (P("dp", "shard", None), P("dp", "shard", None), P())
    out_specs = (P("dp", "shard", None), P())
    return jax.shard_map(
        per_device, mesh=mesh, in_specs=in_specs, out_specs=out_specs, check_vma=False
    )
```

```python
import functools

import jax
import jax.numpy as jnp
from jax import lax
from jax.experimental import pallas as pl
from jax.experimental.pallas import tpu as pltpu
from jax.sharding import PartitionSpec as P

MESH = pl.DeviceIdType.MESH
D = 3968
RANK = 128
ROWS = 384
ZS, YS, XS, CORES = 8, 4, 4, 2
DP = ZS * YS
PIECE = ROWS // DP
PADDED = 4096
HALF = PADDED // CORES
BIG = HALF // 4
HALF_BIG = BIG // 2
PAIR = HALF_BIG // 2
GROUP = PAIR // 2
SMALL = GROUP // ZS
BLOCKS = D // 128
FAR = (2, 1, 3, 0)
FAR_Z = (4, 3, 5, 2, 6, 1, 7, 0)
VMEM_BYTES = 48 * 1024 * 1024
STORE_VMEM = 16 * 1024 * 1024


def eight_columns(live_from, gram, inverse):
    size = gram.shape[0]
    row = lax.broadcasted_iota(jnp.int32, (size, 1), 0)
    row8 = lax.broadcasted_iota(jnp.int32, (8, RANK), 0)
    live = row[8:] < live_from
    columns = [jnp.broadcast_to(gram[:, k:k + 1], (size, RANK)) for k in range(8)]
    top = [column[:8] for column in columns]
    below = [jnp.where(live, column[8:], 0.0) for column in columns]
    gram8, inverse8 = gram[:8], inverse[:8]
    gram_rest, inverse_rest = gram[8:], inverse[8:]
    pivots = []
    for k in range(8):
        pivot = jnp.broadcast_to(top[k][k:k + 1], (8, RANK))
        reciprocal = 1.0 / pivot
        pivots.append(pivot[:1])
        factor8 = jnp.where(row8 > k, top[k] * reciprocal, 0.0)
        factor = below[k] * reciprocal[:1]
        for j in range(k + 1, 8):
            upper = top[j][k:k + 1]
            top[j] = top[j] - factor8 * upper
            below[j] = below[j] - factor * upper
        gram_row, inverse_row = gram8[k:k + 1], inverse8[k:k + 1]
        gram_rest = gram_rest - factor * gram_row
        inverse_rest = inverse_rest - factor * inverse_row
        gram8 = gram8 - factor8 * gram_row
        inverse8 = inverse8 - factor8 * inverse_row
    done = inverse8 * lax.rsqrt(jnp.concatenate(pivots, 0))
    gram = pltpu.roll(jnp.concatenate([gram_rest, gram8], 0), RANK - 8, 1)
    return gram, jnp.concatenate([inverse_rest, inverse8], 0), done


def split(value):
    high = value.astype(jnp.bfloat16)
    return high, (value - high.astype(jnp.float32)).astype(jnp.bfloat16)


def land(ref, sem):
    pltpu.make_async_copy(ref, ref, sem).wait()


def exchange_kernel(g_hbm, m_hbm, f_hbm, new_ref, n_ref,
                    gm, f, gmt, part, part_y, part_z, span_all, span, span2, o2,
                    gram, gram_in, gram_x, gram_back, lower, work, inverse, x, core_in, a_in, z_in,
                    load_sem, party_send, party_recv, part_send, part_recv, span_send, span_recv,
                    gram_send, gram_recv, core_send, core_recv, a_send, a_recv, z_send, z_recv,
                    gz_send, gz_recv, ga_send, ga_recv, gc_send, gc_recv):
    dp, shard = lax.axis_index("dp"), lax.axis_index("shard")
    zi, yi = dp // YS, dp % YS
    xi, ci = shard // CORES, shard % CORES
    a = xi * (1 - ci) + yi * ci
    b = yi * (1 - ci) + xi * ci

    def plane_peer(j):
        return (j, shard)

    def a_peer(k):
        return (zi * YS + (yi + k * ci) % 4, ((xi + k * (1 - ci)) % 4) * CORES + ci)

    def y_peer(k):
        return (zi * YS + (yi + k) % YS, shard)

    def bz_peer(flip, kz):
        at = flipped(b, flip)
        return (((zi + kz) % ZS) * YS + yi * ci + at * (1 - ci), (xi * (1 - ci) + at * ci) * CORES + ci)

    def xz_peer(kx, kz):
        return (((zi + kz) % ZS) * YS + yi, ((xi + kx) % 4) * CORES + ci)

    sibling = (dp, xi * CORES + 1 - ci)

    def send(src, dst, send_sem, recv_sem, to):
        pltpu.make_async_remote_copy(src_ref=src, dst_ref=dst, send_sem=send_sem, recv_sem=recv_sem,
                                     device_id=to, device_id_type=MESH).start()

    def greet(to):
        pl.semaphore_signal(barrier, inc=1, device_id=to, device_id_type=MESH)


    def quarter(i):
        return (yi + FAR[i]) % 4

    def loads(i):
        q = quarter(i)
        rows = pl.ds(pl.multiple_of(q * 96, 96), 96)
        first = pl.ds(pl.multiple_of(q * 192, 96), 96)
        second = pl.ds(pl.multiple_of(q * 192 + 96, 96), 96)
        return (pltpu.make_async_copy(g_hbm.at[rows], gm.at[first], load_sem.at[2 * i]),
                pltpu.make_async_copy(m_hbm.at[rows], gm.at[second], load_sem.at[2 * i + 1]))

    load_f = pltpu.make_async_copy(f_hbm, f, load_sem.at[8])
    load_f.start()
    for i in range(2):
        for copy in loads(i):
            copy.start()

    barrier = pltpu.get_barrier_semaphore()
    for k in (4, 3, 5, 2, 6, 1, 7):
        greet(xz_peer(0, k))
    for k in (2, 1, 3):
        greet(y_peer(k))
        greet(xz_peer(k, 0))
    greet(sibling)

    load_f.wait()
    for i in range(4):
        q = quarter(i)
        for copy in loads(i):
            copy.wait()
        if i < 2:
            for copy in loads(i + 2):
                copy.start()
        both = jnp.dot(gm[pl.ds(pl.multiple_of(q * 192, 192), 192), :], f[...], preferred_element_type=jnp.float32)
        value = both[:96] + both[96:]
        for j in range(ZS):
            part[q * ZS + j] = value[PIECE * j:PIECE * (j + 1)]
        if i == 0:
            pl.semaphore_wait(barrier, 14)
        if FAR[i]:
            send(part.at[pl.ds(q * ZS, ZS)], part_y.at[i], party_send, party_recv.at[i], y_peer(FAR[i]))

    def turn(i, _):
        lanes = pl.ds(pl.multiple_of(i * 128, 128), 128)
        gmt[lanes, :] = gm[:, lanes].T
        return 0
    lax.fori_loop(0, BLOCKS // 2, turn, 0)
    for i in range(3):
        land(part_y.at[i], party_recv.at[i])
    for j in range(ZS):
        to = (zi + FAR_Z[j]) % ZS
        slot = yi * ZS + to
        part[slot] = (part[slot] + part_y[0, to]) + (part_y[1, to] + part_y[2, to])
        if FAR_Z[j]:
            send(part.at[slot], part_z.at[FAR_Z[j] - 1], part_send, part_recv, xz_peer(0, FAR_Z[j]))
    lax.fori_loop(BLOCKS // 2, BLOCKS, turn, 0)
    gmt[D:, :] = jnp.zeros((PADDED - D, 2 * ROWS), jnp.bfloat16)

    me = yi * ZS + zi
    land(part_z, part_recv)
    total = part[me]
    for k in range(ZS - 1):
        total = total + part_z[k]
    span_all[me] = total * (1.0 / DP)

    def spread(k, _):
        send(span_all.at[me], span_all.at[me], span_send, span_recv, plane_peer((dp + k) % DP))
        return 0
    lax.fori_loop(10, 23, spread, 0)
    lax.fori_loop(1, 10, spread, 0)
    lax.fori_loop(23, DP, spread, 0)
    land(span_all.at[pl.ds(0, DP - 1)], span_recv)

    for j in range(DP // 2):
        span[24 * j:24 * (j + 1), :] = jnp.concatenate([span_all[2 * j], span_all[2 * j + 1]], 0)
    for q in range(4):
        high, low = split(span[96 * q:96 * (q + 1), :])
        for start in (192 * q, 192 * q + 96):
            span2[start:start + 96, :RANK] = high
            span2[start:start + 96, RANK:] = low

    mine = pl.ds(pl.multiple_of(ci * 64, 64), 64)
    other = pl.ds(pl.multiple_of((1 - ci) * 64, 64), 64)

    def product(start, size=BIG):
        both = jnp.dot(gmt[pl.ds(start, size), :], span2[...], preferred_element_type=jnp.float32)
        return both[:, :RANK] + both[:, RANK:]

    def for_sibling(i):
        start = pl.multiple_of((1 - ci) * HALF + ((b + FAR[i]) % 4) * BIG, BIG)
        if i == 0:
            for half in (0, 1):
                rows = pl.ds(pl.multiple_of(start + half * HALF_BIG, HALF_BIG), HALF_BIG)
                x[rows, :] = product(rows.start, HALF_BIG)
                send(x.at[rows], core_in.at[0, pl.ds(half * HALF_BIG, HALF_BIG)], core_send, core_recv.at[4 * half],
                     sibling)
            return
        x[pl.ds(start, BIG), :] = product(start)
        send(x.at[pl.ds(start, BIG)], core_in.at[i], core_send, core_recv.at[i], sibling)

    def pair_of(core, first, half, pair):
        return pl.multiple_of(core * HALF + first * BIG + half * HALF_BIG + pair * PAIR, PAIR)

    def group_of(core, first, half, second):
        return pl.multiple_of(core * HALF + first * BIG + half * HALF_BIG + second * GROUP, GROUP)

    def flipped(place, flip):
        return (place // 2 + flip // 2) % 2 * 2 + (place + flip) % 2

    def to_axis(i, half):
        for flip in (3, 2, 1, 0):
            rows = pl.ds(group_of(ci, (a + FAR[i]) % 4, half, flipped(b, flip)), GROUP)
            send(x.at[rows], a_in.at[i, half, flip], a_send, a_recv.at[i, half, flip], a_peer(FAR[i]))

    def for_axis(i):
        start = pl.multiple_of(ci * HALF + ((a + FAR[i]) % 4) * BIG, BIG)
        if i == 0:
            for half in (0, 1):
                rows = pl.ds(pl.multiple_of(start + half * HALF_BIG, HALF_BIG), HALF_BIG)
                part_in = pl.ds(half * HALF_BIG, HALF_BIG)
                value = product(rows.start, HALF_BIG)
                land(core_in.at[0, part_in], core_recv.at[4 * half])
                x[rows, :] = value + core_in[0, part_in, :]
                if half == 0:
                    to_axis(i, 0)
            return
        value = product(start)
        land(core_in.at[i], core_recv.at[i])
        x[pl.ds(start, BIG), :] = value + core_in[i]
        if FAR[i]:
            to_axis(i, 0)

    gram[...] = lax.dot_general(span[...], span[...], (((0,), (0,)), ((), ())),
                                precision=lax.Precision.HIGHEST, preferred_element_type=jnp.float32)
    send(gram.at[other], gram_in, gram_send.at[0], gram_recv.at[0], sibling)
    for_sibling(0)
    for_sibling(1)
    land(gram_in, gram_recv.at[0])
    gram[mine, :] = gram[mine, :] + gram_in[...]
    for r in (1, 2, 3):
        send(gram.at[mine], gram_x.at[r - 1], gram_send.at[1], gram_recv.at[1], xz_peer(r, 0))
    for_axis(0)
    for_sibling(2)
    for_axis(1)
    for_sibling(3)
    for_axis(2)
    for i in range(3):
        to_axis(i, 1)
    for_axis(3)
    row = lax.broadcasted_iota(jnp.int32, (RANK, RANK), 0)
    lane = lax.broadcasted_iota(jnp.int32, (RANK, RANK), 1)
    work[...] = (row == lane).astype(jnp.float32)

    def eliminate(first, last):
        size = RANK - 32 * (first // 4)

        def one(step, _):
            rows = pl.ds(pl.multiple_of(step * 8, 8), 8)
            lower[:size, :], work[:size, :], inverse[rows, :] = eight_columns(
                RANK - 8 * step, lower[:size, :], work[:size, :])
            return 0
        lax.fori_loop(first, last, one, 0)

    def to_owners(half, flip):
        block = group_of(ci, a, half, flipped(b, flip))
        rows = pl.ds(block, GROUP)
        for i in range(3):
            land(a_in.at[i, half, flip], a_recv.at[i, half, flip])
        x[rows, :] = x[rows, :] + a_in[0, half, flip] + a_in[1, half, flip] + a_in[2, half, flip]
        for kz in FAR_Z:
            if flip or kz:
                piece = pl.ds(pl.multiple_of(block + (zi + kz) % ZS * SMALL, SMALL), SMALL)
                slot = ZS * (3 - flip) + kz - (1 if flip == 0 else 0)
                send(x.at[piece], z_in.at[half, slot], z_send, z_recv.at[half], bz_peer(flip, kz))

    to_owners(0, 3)
    to_owners(0, 2)
    land(gram_x, gram_recv.at[1])
    land(gram_x, gram_send.at[1])
    gram[mine, :] = gram[mine, :] + gram_x[0] + gram_x[1] + gram_x[2]
    send(gram.at[mine], gram_back, gram_send.at[2], gram_recv.at[2], sibling)
    lower[mine, :] = gram[mine, :]
    to_owners(0, 1)
    to_owners(0, 0)
    land(gram_back, gram_recv.at[2])
    lower[other, :] = gram_back[...]
    eliminate(0, 1)
    to_owners(1, 3)
    eliminate(1, 2)
    to_owners(1, 2)
    eliminate(2, 3)
    to_owners(1, 1)
    eliminate(3, 4)
    to_owners(1, 0)
    eliminate(4, 8)
    eliminate(8, 12)
    eliminate(12, 16)

    def spread_rows(half):
        rows = pl.ds(pl.multiple_of(group_of(ci, a, half, b) + zi * SMALL, SMALL), SMALL)
        land(z_in.at[half], z_recv.at[half])
        total = x[rows, :]
        for k in range(4 * ZS - 1):
            total = total + z_in[half, k]
        n_ref[rows, :] = lax.dot_general(total * (1.0 / DP), inverse[...], (((1,), (1,)), ((), ())),
                                         precision=lax.Precision.HIGHEST, preferred_element_type=jnp.float32)
        for flip in range(4):
            for kz in FAR_Z:
                if flip or kz:
                    send(n_ref.at[rows], n_ref.at[rows], gz_send, gz_recv.at[half, flip], bz_peer(flip, kz))

    spread_rows(0)
    span_in_basis = lax.dot_general(span[...], inverse[...], (((1,), (1,)), ((), ())),
                                    precision=lax.Precision.HIGHEST, preferred_element_type=jnp.float32)
    high, low = split(span_in_basis)
    o2[:, :RANK] = high
    o2[:, RANK:] = low
    spread_rows(1)

    def residual(start, width):
        @pl.when(start < D)
        def _():
            cols = pl.ds(start, width)
            high, low = split(n_ref[cols, :])
            update = (lax.dot_general(o2[...], jnp.concatenate([high, high], 1), (((1,), (1,)), ((), ())),
                                      preferred_element_type=jnp.float32)
                      + lax.dot_general(o2[:, :RANK], low, (((1,), (1,)), ((), ())),
                                        preferred_element_type=jnp.float32))
            for q in range(4):
                corrected = (gm[192 * q:192 * q + 96, cols].astype(jnp.float32)
                             + gm[192 * q + 96:192 * q + 192, cols].astype(jnp.float32))
                new_ref[96 * q:96 * (q + 1), cols] = (corrected - update[96 * q:96 * (q + 1)]).astype(jnp.bfloat16)

    def from_owners(half, flip):
        rows = pl.ds(group_of(ci, a, half, flipped(b, flip)), GROUP)
        land(n_ref.at[pl.ds(0, GROUP - (SMALL if flip == 0 else 0))], gz_recv.at[half, flip])
        for r in range(3):
            send(n_ref.at[rows], n_ref.at[rows], ga_send, ga_recv.at[r, half, flip], a_peer(FAR[r]))
        send(n_ref.at[rows], n_ref.at[rows], gc_send, gc_recv.at[3, half, flip], sibling)

    def from_axis(half, flip):
        for i in (1, 2, 0):
            rows = pl.ds(group_of(ci, (a - FAR[i] + 4) % 4, half, flipped(b, flip)), GROUP)
            land(n_ref.at[rows], ga_recv.at[i, half, flip])
            send(n_ref.at[rows], n_ref.at[rows], gc_send, gc_recv.at[i, half, flip], sibling)

    def from_sibling(i, half, flips):
        for flip in flips:
            land(n_ref.at[pl.ds(0, GROUP)], gc_recv.at[i, half, flip])

    DISTANCES = FAR[:3] + (0,)

    def whole(core, first, half):
        start = pl.multiple_of(pair_of(core, first, half, 0), HALF_BIG)
        if half == 0:
            residual(start, HALF_BIG)
        else:
            @pl.when(start + HALF_BIG <= D)
            def _():
                residual(start, HALF_BIG)

            @pl.when(start + HALF_BIG > D)
            def _():
                residual(pl.multiple_of(start, PAIR), PAIR)

    def own_columns(i, half):
        whole(ci, (a - DISTANCES[i] + 4) % 4, half)

    def sibling_columns(i, half):
        whole(1 - ci, (b - DISTANCES[i] + 4) % 4, half)

    from_owners(0, 0)
    from_owners(0, 1)
    from_owners(1, 0)
    from_owners(0, 2)
    from_owners(0, 3)
    from_axis(0, 0)
    own_columns(3, 0)
    from_owners(1, 1)
    from_axis(0, 1)
    from_owners(1, 2)
    from_axis(1, 0)
    from_owners(1, 3)
    own_columns(3, 1)
    from_axis(0, 2)
    from_axis(0, 3)
    for i in range(3):
        own_columns(i, 0)
    from_axis(1, 1)
    for i in (3, 1, 2, 0):
        from_sibling(i, 0, range(4))
        sibling_columns(i, 0)
    from_axis(1, 2)
    from_axis(1, 3)
    from_sibling(3, 1, range(4))
    sibling_columns(3, 1)
    for i in range(3):
        own_columns(i, 1)
    for i in (1, 2, 0):
        from_sibling(i, 1, range(4))
        sibling_columns(i, 1)

    land(part_y, party_send)
    land(part_z, part_send)
    land(span_all.at[pl.ds(0, DP - 1)], span_send)
    land(gram_in, gram_send.at[0])
    land(gram_in, gram_send.at[2])
    land(x.at[pl.ds(0, HALF)], core_send)
    land(a_in, a_send)
    land(z_in, z_send)
    land(z_in, gz_send)
    land(a_in, ga_send)
    land(x.at[pl.ds(0, HALF)], gc_send)


def exchange(g, m, f):
    dma = pltpu.SemaphoreType.DMA
    f32, bf16 = jnp.float32, jnp.bfloat16
    return pl.pallas_call(
        exchange_kernel,
        out_shape=(jax.ShapeDtypeStruct((ROWS, D), bf16), jax.ShapeDtypeStruct((PADDED, RANK), f32)),
        in_specs=[pl.BlockSpec(memory_space=pltpu.HBM)] * 3,
        out_specs=(pl.BlockSpec(memory_space=pltpu.VMEM), pl.BlockSpec(memory_space=pltpu.VMEM)),
        scratch_shapes=[
            pltpu.VMEM((2 * ROWS, D), bf16), pltpu.VMEM((D, RANK), bf16), pltpu.VMEM((PADDED, 2 * ROWS), bf16),
            pltpu.VMEM((DP, PIECE, RANK), f32), pltpu.VMEM((3, ZS, PIECE, RANK), f32),
            pltpu.VMEM((ZS - 1, PIECE, RANK), f32),
            pltpu.VMEM((DP, PIECE, RANK), f32), pltpu.VMEM((ROWS, RANK), f32),
            pltpu.VMEM((2 * ROWS, 2 * RANK), bf16), pltpu.VMEM((ROWS, 2 * RANK), bf16),
            pltpu.VMEM((RANK, RANK), f32), pltpu.VMEM((64, RANK), f32), pltpu.VMEM((3, 64, RANK), f32),
            pltpu.VMEM((64, RANK), f32), pltpu.VMEM((RANK, RANK), f32), pltpu.VMEM((RANK, RANK), f32),
            pltpu.VMEM((RANK, RANK), f32),
            pltpu.VMEM((PADDED, RANK), f32), pltpu.VMEM((4, BIG, RANK), f32),
            pltpu.VMEM((3, 2, 4, GROUP, RANK), f32), pltpu.VMEM((2, 4 * ZS - 1, SMALL, RANK), f32),
            dma((9,)), dma, dma((3,)), dma, dma, dma, dma, dma((3,)), dma((3,)), dma, dma((5,)), dma, dma((3, 2, 4)), dma, dma((2,)),
            dma, dma((2, 4)), dma, dma((3, 2, 4)), dma, dma((4, 2, 4)),
        ],
        compiler_params=pltpu.CompilerParams(collective_id=0, has_side_effects=True, vmem_limit_bytes=VMEM_BYTES),
        name="exchange",
    )(g, m, f)


def store_kernel(new_ref, n_ref, memory_ref, factor_ref, sems):
    copies = [pltpu.make_async_copy(new_ref.at[pl.ds(96 * i, 96)], memory_ref.at[pl.ds(96 * i, 96)], sems.at[i])
              for i in range(4)]
    quarter = D // 4
    copies += [pltpu.make_async_copy(n_ref.at[pl.ds(quarter * i, quarter)], factor_ref.at[pl.ds(quarter * i, quarter)],
                                     sems.at[4 + i]) for i in range(4)]
    for copy in copies:
        copy.start()
    for copy in copies:
        copy.wait()


def store(new, n):
    return pl.pallas_call(
        store_kernel,
        out_shape=(jax.ShapeDtypeStruct((ROWS, D), jnp.bfloat16), jax.ShapeDtypeStruct((D, RANK), jnp.float32)),
        in_specs=[pl.BlockSpec(memory_space=pltpu.VMEM)] * 2,
        out_specs=(pl.BlockSpec(memory_space=pltpu.HBM), pl.BlockSpec(memory_space=pltpu.HBM)),
        scratch_shapes=[pltpu.SemaphoreType.DMA((8,))],
        compiler_params=pltpu.CompilerParams(vmem_limit_bytes=STORE_VMEM),
        name="store",
    )(new, n)


def per_device(gradient, memory, old_factor):
    new_memory, new_factor = store(*exchange(gradient[0], memory[0], pltpu.with_memory_space_constraint(old_factor, pltpu.HBM)))
    return (new_memory[None], new_factor)


def solution(mesh):
    in_specs = (P("dp", "shard", None), P("dp", "shard", None), P())
    out_specs = (P("dp", "shard", None), P())
    return jax.shard_map(
        per_device, mesh=mesh, in_specs=in_specs, out_specs=out_specs, check_vma=False
    )
```
